128 devices in a mesh: view: 8 (over x, z_lo), seq: 16 (over y, z_hi, core).
Axes of the slice: x: 4, y: 4, z: 4 (z_hi: 2, z_lo: 2; z = z_hi * 2 + z_lo), core: 2. Of those that a mesh axis runs over, the one named last changes fastest.
Arguments:
- target: bfloat16 [8, 2048, 2048], P('view', 'seq'), may hold values from -6 to 6
- ref_slots: bfloat16 [8, 2048, 2048], P('view', 'seq'), may hold values from -6 to 6
- owners: int32 [4], replicated, may hold values from 0 to 7, as said below
- norm_gain: float32 [2048], replicated, may hold values from 0.1 to 1.9
- w_qkv: bfloat16 [2048, 3, 2048], P(None, None, 'seq'), may hold values from -0.125 to 0.125
- head_scale: float32 [16], P('seq'), may hold values from 1.5 to 40
- w_out: bfloat16 [2048, 2048], P('seq'), may hold values from -0.5 to 0.5
Outputs:
- output: bfloat16 [8, 2048, 2048], P('view', 'seq')
The draws below stay inside these ranges and needn't reach their ends.
Inputs may be any that keep to these rules, and one draw needn't show every extreme that they name: `owners`: the 4 entries are distinct slots; slot 0 and slot 7 are always among them.
All inputs are finite; a program needn't handle non-finite values.
Results may differ from the reference program's by a relative error of at most 0.02.
The reference program's roundings to bfloat16 on the way (of `normed`, `slot_normed`, `qkv`, `ref_kv`, `weights` and `attended`) count: a program that leaves them out, or rounds other values in their place, can miss the bound.
Values may be sent and summed in bfloat16 or wider, within the bound.
A program may use at most 128 MiB of HBM per device.

```python
import math
import jax
import jax.numpy as jnp
from jax import lax

D = 2048
H = 16
HD = 128
LEN = 2048
REFS = 4
VIEWS = 8
SLOTS = 8


def draw_owners(key, part):
    key = jax.random.fold_in(key, 7)
    middle_key, order_key = jax.random.split(key)
    middle = 1 + jax.random.permutation(middle_key, SLOTS - 2)[:REFS - 2].astype(jnp.int32)
    ends = jnp.array([0, SLOTS - 1], jnp.int32)
    chosen = jnp.concatenate([ends, middle], axis=0)
    return jax.random.permutation(order_key, chosen).astype(jnp.int32)


def draw_head_scale(key, part):
    key = jax.random.fold_in(key, 11)
    low_key = jax.random.fold_in(key, 0)
    logs = jax.random.uniform(low_key, (H,), jnp.float32, math.log(1.5), math.log(4.0))
    return jnp.exp(logs)


def steps_of(key, dims, pieces, smallest, high):
    level, own = 1.0, jax.random.fold_in(key, 6)
    for position, shards_of in pieces:
        steps = jnp.exp(jax.random.uniform(jax.random.fold_in(own, position), (shards_of,), jnp.float32, smallest / len(pieces), high / len(pieces)))
        level = level * jnp.repeat(steps, dims[position] // shards_of).reshape([-1 if axis == position else 1 for axis in range(len(dims))])
    return level


def noise(stream_key, extent, width, bound, cuts=(), kind=jnp.bfloat16):
    result = width * jax.random.normal(stream_key, extent, jnp.float32)
    if cuts:
        result = result * steps_of(stream_key, extent, cuts, -0.22, 0.18)
    return jnp.clip(result, -bound, bound).astype(kind)


def setup_inputs(seed: int = 0) -> dict:
    arg_keys = jax.random.split(jax.random.key(seed), 8)
    return {
        "target": noise(arg_keys[0], (VIEWS, LEN, D), 1.0, 6.0, ((0, 8), (1, 16))),
        "ref_slots": noise(arg_keys[1], (SLOTS, LEN, D), 1.0, 6.0, ((0, 8), (1, 16))),
        "owners": draw_owners(jax.random.fold_in(arg_keys[7], 71), 0),
        "norm_gain": jnp.clip(1.0 + 0.18 * jax.random.normal(arg_keys[3], (D,), jnp.float32), 0.1, 1.9),
        "w_qkv": noise(arg_keys[4], (D, 3, H * HD), D ** -0.5, 0.125, ((2, 16),)),
        "head_scale": draw_head_scale(jax.random.fold_in(arg_keys[7], 71), 0),
        "w_out": noise(arg_keys[6], (H * HD, D), HD ** -0.5, 0.5, ((0, 16),)),
    }


def rms_norm(x, gain):
    xf = x.astype(jnp.float32)
    scaled = xf * lax.rsqrt(lax.optimization_barrier(jnp.mean(xf * xf, axis=-1, keepdims=True)) + 1e-06)
    return (scaled * gain.astype(jnp.float32)).astype(jnp.bfloat16)

def attend_heads(query, keys, values, scale):

    def one_head(packed):
        qh, kh, vh, sh = packed
        scores = jnp.dot(qh, kh.T, preferred_element_type=jnp.float32) * (sh * HD ** (-0.5))
        top = lax.optimization_barrier(jnp.max(scores, axis=-1, keepdims=True))
        expo = jnp.exp(scores - top)
        weights = (expo / lax.optimization_barrier(jnp.sum(expo, axis=-1, keepdims=True))).astype(jnp.bfloat16)
        return jnp.dot(weights, vh, preferred_element_type=jnp.float32).astype(jnp.bfloat16)
    return lax.map(one_head, (query, keys, values, scale))

def reference(target, ref_slots, owners, norm_gain, w_qkv, head_scale, w_out):
    normed = rms_norm(target, norm_gain)
    qkv = jnp.dot(normed.reshape(-1, D), w_qkv.reshape(D, -1), preferred_element_type=jnp.float32)
    qkv = qkv.astype(jnp.bfloat16).reshape(VIEWS, LEN, 3, H, HD)
    chosen = ref_slots[owners.astype(jnp.int32)]
    slot_normed = rms_norm(chosen, norm_gain)
    ref_kv = jnp.dot(slot_normed.reshape(-1, D), w_qkv[:, 1:, :].reshape(D, -1), preferred_element_type=jnp.float32)
    ref_kv = ref_kv.astype(jnp.bfloat16).reshape(REFS * LEN, 2, H, HD)
    ref_keys = jnp.transpose(ref_kv[:, 0], (1, 0, 2))
    ref_values = jnp.transpose(ref_kv[:, 1], (1, 0, 2))

    def one_view(view_qkv):
        query = jnp.transpose(view_qkv[:, 0], (1, 0, 2))
        keys = jnp.concatenate([jnp.transpose(view_qkv[:, 1], (1, 0, 2)), ref_keys], axis=1)
        values = jnp.concatenate([jnp.transpose(view_qkv[:, 2], (1, 0, 2)), ref_values], axis=1)
        heads = attend_heads(query, keys, values, head_scale)
        return jnp.transpose(heads, (1, 0, 2)).reshape(LEN, H * HD)
    attended = lax.map(one_view, qkv)
    output = jnp.dot(attended.reshape(-1, H * HD), w_out, preferred_element_type=jnp.float32)
    return output.astype(jnp.bfloat16).reshape(VIEWS, LEN, D)
```

```python
import math

import jax
import jax.numpy as jnp
from jax import lax
from jax.experimental import pallas as pl
from jax.experimental.pallas import tpu as pltpu
from jax.sharding import PartitionSpec as P

HD = 128
D = 2048
LEN = 2048
TB = 128
SB = 64
RC = 1024
QB = 512
MESH = pl.DeviceIdType.MESH
F32 = jnp.float32
BF16 = jnp.bfloat16
NT = (((1,), (1,)), ((), ()))


def rows(start, size):
    return pl.ds(pl.multiple_of(start, size), size)


def normalise(x, gain):
    xf = x.astype(F32)
    scaled = xf * lax.rsqrt(jnp.mean(xf * xf, axis=-1, keepdims=True) + 1e-06)
    return (scaled * gain).astype(BF16)


class Gather:
    def __init__(self, buf, size, place, me, ring, partner, sibling, send, recv):
        self.buf, self.size, self.place = buf, size, place
        self.pos, self.side = me
        self.ring, self.partner, self.sibling = ring, partner, sibling
        self.send, self.recv = send, recv
        self.started = []

    def region(self, shift, k, half=None):
        pos = lax.rem(self.pos + shift, 4)
        side = self.side if k == 0 else 1 - self.side
        start = self.place(pos, side) * self.size
        if half is None:
            return self.buf.at[rows(start, self.size)]
        part = self.size // 2
        return self.buf.at[rows(start + half * part, part)]

    def put(self, region, device, sem):
        copy = pltpu.make_async_remote_copy(
            src_ref=region,
            dst_ref=region,
            send_sem=self.send.at[len(self.started)],
            recv_sem=self.recv.at[sem],
            device_id=device,
            device_id_type=MESH,
        )
        copy.start()
        self.started.append(copy)

    def got(self, region, sem):
        pltpu.make_async_remote_copy(
            src_ref=region,
            dst_ref=region,
            send_sem=self.send.at[0],
            recv_sem=self.recv.at[sem],
            device_id=self.partner,
            device_id_type=MESH,
        ).wait_recv()

    def share(self, shift, k):
        if self.sibling is not None:
            self.put(self.region(shift, k), self.sibling, 9 + {0: 0, 3: 2, 1: 4, 2: 6}[shift] + k)

    def own(self):
        block = self.region(0, 0)
        self.put(block, self.partner, 0)
        self.put(block, self.ring[0], 1)
        self.put(block, self.ring[1], 3)
        self.share(0, 0)

    def wait_partner(self):
        self.got(self.region(0, 1), 0)

    def pass_partner(self):
        block = self.region(0, 1)
        self.put(block, self.ring[0], 2)
        self.put(block, self.ring[1], 4)
        self.share(0, 1)

    def on_below(self, k):
        self.got(self.region(3, k), 1 + k)
        self.put(self.region(3, k, 0), self.ring[0], 5 + k)
        self.share(3, k)

    def on_above(self, k):
        self.got(self.region(1, k), 3 + k)
        self.put(self.region(1, k, 1), self.ring[1], 7 + k)
        self.share(1, k)

    def on_far(self, k):
        self.got(self.region(2, k, 0), 5 + k)
        self.got(self.region(2, k, 1), 7 + k)
        self.share(2, k)

    def wait_shared(self, sibling_region):
        for index, shift in enumerate((0, 3, 1, 2)):
            for k in range(2):
                self.got(sibling_region(shift, k), 9 + 2 * index + k)

    def close(self):
        for copy in self.started:
            copy.wait_send()


def kernel(
    x_ref, slot_ref, gain_ref, w_ref, scale_ref, sel_ref, wout_ref, out_ref,
    tok, ref_tok, wo, kv, query, acc, top, att, att_in, keep, give, moved, arrived,
    t_send, t_recv, s_send, s_recv, w_send, w_recv, r_send, r_recv, a_send, a_recv,
    m_send, m_recv,
):
    view, seq = lax.axis_index("view"), lax.axis_index("seq")
    x, zl = view // 2, lax.rem(view, 2)
    y, zh, core = seq // 4, lax.rem(seq // 2, 2), lax.rem(seq, 2)

    def seq_of(y_, zh_, c_):
        return (y_ * 2 + zh_) * 2 + c_

    y_up, y_down = lax.rem(y + 1, 4), lax.rem(y + 3, 4)
    x_up, x_down = lax.rem(x + 1, 4), lax.rem(x + 3, 4)
    seq_ring = ((view, seq_of(y_up, zh, core)), (view, seq_of(y_down, zh, core)))
    seq_partner = (view, seq_of(y, 1 - zh, core))
    sibling = (view, seq_of(y, zh, 1 - core))
    view_ring = ((x_up * 2 + zl, seq), (x_down * 2 + zl, seq))
    view_partner = (x * 2 + 1 - zl, seq)

    peers = []
    for dy in range(4):
        for dz in range(2):
            for dc in range(2):
                if (dy, dz, dc) != (0, 0, 0):
                    zh_ = zh if dz == 0 else 1 - zh
                    c_ = core if dc == 0 else 1 - core
                    peers.append((view, seq_of(lax.rem(y + dy, 4), zh_, c_)))
    peers += [view_partner, view_ring[0], view_ring[1]]
    barrier = pltpu.get_barrier_semaphore()
    for peer in peers:
        pl.semaphore_signal(barrier, inc=1, device_id=peer, device_id_type=MESH)

    def seq_place(y_, zh_):
        return seq_of(y_, zh_, core)

    me = (y, zh)
    g_t = Gather(tok, TB, seq_place, me, seq_ring, seq_partner, sibling, t_send, t_recv)
    g_s = Gather(ref_tok, SB, seq_place, me, seq_ring, seq_partner, sibling, s_send, s_recv)
    g_w = Gather(wo, TB, seq_place, me, seq_ring, seq_partner, sibling, w_send, w_recv)
    g_r = Gather(
        kv, RC, lambda x_, zl_: x_ * 2 + zl_, (x, zl), view_ring, view_partner, None, r_send, r_recv
    )

    def of_sibling(buf, size):
        def region(shift, k):
            zh_ = zh if k == 0 else 1 - zh
            return buf.at[rows(seq_of(lax.rem(y + shift, 4), zh_, 1 - core) * size, size)]

        return region

    gain = gain_ref[...]
    keep[zl] = normalise(slot_ref[rows(zl * SB, SB), :], gain)
    give[...] = normalise(slot_ref[rows((1 - zl) * SB, SB), :], gain)
    pl.semaphore_wait(barrier, len(peers))
    swap = pltpu.make_async_remote_copy(
        src_ref=give, dst_ref=keep.at[zl], send_sem=m_send.at[0], recv_sem=m_recv.at[0],
        device_id=view_partner, device_id_type=MESH,
    )
    swap.start()
    tok[rows(seq * TB, TB), :] = normalise(x_ref[...], gain)
    g_t.own()
    wo[rows(seq * TB, TB), :] = wout_ref[...]

    pltpu.make_async_remote_copy(
        src_ref=give, dst_ref=keep.at[1 - zl], send_sem=m_send.at[0], recv_sem=m_recv.at[0],
        device_id=view_partner, device_id_type=MESH,
    ).wait_recv()
    even, odd = keep[0].astype(F32), keep[1].astype(F32)
    moved[...] = jnp.where(sel_ref[0:1, :] == 0.0, even, odd).astype(BF16)
    half = x // 2
    move = pltpu.make_async_remote_copy(
        src_ref=moved, dst_ref=arrived.at[half], send_sem=m_send.at[1], recv_sem=m_recv.at[1 + half],
        device_id=((x + 1 - 2 * half) * 2 + zl, seq), device_id_type=MESH,
    )
    move.start()
    mine = rows(seq * SB, SB)
    middle = jnp.logical_or(x == 1, x == 2)

    @pl.when(jnp.logical_not(middle))
    def _():
        ref_tok[mine, :] = jnp.where(
            sel_ref[1:2, :] == 0.0, keep[0].astype(F32), keep[1].astype(F32)
        ).astype(BF16)

    @pl.when(middle)
    def _():
        for side in range(2):
            pltpu.make_async_remote_copy(
                src_ref=moved, dst_ref=arrived.at[side], send_sem=m_send.at[1],
                recv_sem=m_recv.at[1 + side], device_id=view_partner, device_id_type=MESH,
            ).wait_recv()
        code = sel_ref[1:2, :]
        near = jnp.where(code == 0.0, keep[0].astype(F32), keep[1].astype(F32))
        far = jnp.where(code == 2.0, arrived[0].astype(F32), arrived[1].astype(F32))
        ref_tok[mine, :] = jnp.where(code < 1.5, near, far).astype(BF16)

    g_s.own()
    g_t.on_below(0)
    g_t.on_above(0)
    g_s.wait_partner()
    g_s.pass_partner()
    g_t.wait_partner()
    g_t.pass_partner()
    g_s.on_below(0)
    g_s.on_above(0)
    g_s.on_below(1)
    g_s.on_above(1)
    g_s.on_far(0)
    g_s.on_far(1)
    g_s.wait_shared(of_sibling(ref_tok, SB))

    def ref_project(i, _):
        own_kv = jnp.dot(ref_tok[rows(i * QB, QB), :], w_ref[:, HD:], preferred_element_type=F32)
        kv[rows(view * RC + i * QB, QB), :] = own_kv.astype(BF16)
        return 0

    lax.fori_loop(0, RC // QB, ref_project, 0)
    g_r.own()
    g_t.on_below(1)
    g_t.on_above(1)
    g_t.on_far(0)
    g_t.on_far(1)
    g_t.wait_shared(of_sibling(tok, TB))
    g_w.own()
    factor = scale_ref[...]

    def project(i, _):
        at = rows(i * QB, QB)
        qkv = jnp.dot(tok[at, :], w_ref[...], preferred_element_type=F32).astype(BF16)
        kv[rows(4 * LEN + i * QB, QB), :] = qkv[:, HD:]
        scaled = qkv[:, :HD].astype(F32) * factor
        high = scaled.astype(BF16)
        low = (scaled - high.astype(F32)).astype(BF16)
        query[at, :] = jnp.concatenate([high, low], axis=1)
        return 0

    lax.fori_loop(0, LEN // QB, project, 0)

    def attend(chunk, first, last):
        at = rows(chunk * LEN, LEN)
        keys, values = kv[at, :HD], kv[at, HD:]
        keys = jnp.concatenate([keys, keys], axis=1)
        values = jnp.concatenate([values, jnp.ones((LEN, HD), BF16)], axis=1)

        def block(t):
            return rows(lax.rem(y + 1 + t, 4) * QB, QB)

        def score(t):
            return lax.dot_general(query[block(t), :], keys, NT, preferred_element_type=F32)

        ahead = score(0)
        for t in range(LEN // QB):
            scores = ahead
            if t + 1 < LEN // QB:
                ahead = score(t + 1)
            q = block(t)
            peak = jnp.max(scores, axis=1, keepdims=True)
            if first:
                new = jnp.broadcast_to(peak, (QB, HD))
            else:
                old = top[q, :]
                new = jnp.maximum(old, peak)
            weights = jnp.exp2(scores - jnp.tile(new, (1, LEN // HD))).astype(BF16)
            total = jnp.dot(weights, values, preferred_element_type=F32)
            if not first:
                total += acc[q, :] * jnp.tile(jnp.exp2(old - new), (1, 2))
            if last:
                att[q, :] = (total[:, :HD] / total[:, HD:]).astype(BF16)
                last(t)
            else:
                top[q, :] = new
                acc[q, :] = total

    sent = []

    def hand_out(t):
        y_ = lax.rem(y + 1 + t, 4)
        for combo in range(4):
            zh_ = zh if combo < 2 else 1 - zh
            c_ = core if combo % 2 == 0 else 1 - core
            to = seq_of(y_, zh_, c_)
            if t == 3 and combo == 0:
                att_in[:, rows(seq * HD, HD)] = att[rows(seq * TB, TB), :]
                continue
            copy = pltpu.make_async_remote_copy(
                src_ref=att.at[rows(to * TB, TB)],
                dst_ref=att_in.at[:, rows(seq * HD, HD)],
                send_sem=a_send.at[t * 4 + combo],
                recv_sem=a_recv.at[t * 4 + combo],
                device_id=(view, to),
                device_id_type=MESH,
            )
            copy.start()
            sent.append(copy)

    g_r.wait_partner()
    g_r.pass_partner()
    attend(4, True, None)
    g_r.on_below(0)
    g_r.on_above(0)
    g_w.wait_partner()
    g_w.pass_partner()
    g_w.on_below(0)
    g_w.on_above(0)
    attend(x, False, None)
    g_r.on_below(1)
    g_r.on_above(1)
    attend(x_down, False, None)
    g_w.on_below(1)
    g_w.on_above(1)
    attend(x_up, False, None)
    g_w.on_far(0)
    g_w.on_far(1)
    g_r.on_far(0)
    g_r.on_far(1)
    attend(lax.rem(x + 2, 4), False, hand_out)

    g_w.wait_shared(of_sibling(wo, TB))
    for t in range(4):
        for combo in range(4):
            if t == 3 and combo == 0:
                continue
            y_ = lax.rem(y + 3 - t, 4)
            zh_ = zh if combo < 2 else 1 - zh
            c_ = core if combo % 2 == 0 else 1 - core
            pltpu.make_async_remote_copy(
                src_ref=att.at[rows(0, TB)],
                dst_ref=att_in.at[:, rows(seq_of(y_, zh_, c_) * HD, HD)],
                send_sem=a_send.at[0],
                recv_sem=a_recv.at[t * 4 + combo],
                device_id=sibling,
                device_id_type=MESH,
            ).wait_recv()

    def output(i, _):
        at = rows(i * QB, QB)
        out_ref[:, at] = jnp.dot(att_in[...], wo[:, at], preferred_element_type=F32).astype(BF16)
        return 0

    lax.fori_loop(0, D // QB, output, 0)
    swap.wait_send()
    move.wait_send()
    for gather in (g_t, g_s, g_w, g_r):
        gather.close()
    for copy in sent:
        copy.wait_send()


def local(target, ref_slots, owners, norm_gain, w_qkv, head_scale, w_out):
    x = lax.axis_index("view") // 2
    inner = jnp.logical_and(owners > 0, owners < 7)
    low = jnp.min(jnp.where(inner, owners, 99))
    high = jnp.max(jnp.where(inner, owners, -1))
    send = jnp.where(
        x == 0, 1, jnp.where(x == 1, jnp.where(high == 2, 0, 1), jnp.where(x == 2, jnp.where(low == 4, 0, 1), 0))
    )
    for_low = jnp.where(low == 1, 2, jnp.where(low == 2, 0, jnp.where(low == 3, 1, 3)))
    for_high = jnp.where(high == 6, 3, jnp.where(high == 4, 0, jnp.where(high == 5, 1, 2)))
    final = jnp.where(x == 0, 0, jnp.where(x == 1, for_low, jnp.where(x == 2, for_high, 1)))
    row = jnp.arange(8)[:, None]
    sel = jnp.broadcast_to(jnp.where(row == 0, send, final).astype(F32), (8, D))
    factor = jnp.broadcast_to((head_scale * (HD ** (-0.5) * math.log2(math.e)))[:, None], (1, HD))
    vmem = pl.BlockSpec(memory_space=pltpu.VMEM)
    dma = pltpu.SemaphoreType.DMA
    out = pl.pallas_call(
        kernel,
        out_shape=jax.ShapeDtypeStruct((TB, D), BF16),
        in_specs=[vmem] * 7,
        out_specs=vmem,
        scratch_shapes=[
            pltpu.VMEM((LEN, D), BF16),
            pltpu.VMEM((RC, D), BF16),
            pltpu.VMEM((D, D), BF16),
            pltpu.VMEM((5 * LEN, 2 * HD), BF16),
            pltpu.VMEM((LEN, 2 * HD), BF16),
            pltpu.VMEM((LEN, 2 * HD), F32),
            pltpu.VMEM((LEN, HD), F32),
            pltpu.VMEM((LEN, HD), BF16),
            pltpu.VMEM((TB, D), BF16),
            pltpu.VMEM((2, SB, D), BF16),
            pltpu.VMEM((SB, D), BF16),
            pltpu.VMEM((SB, D), BF16),
            pltpu.VMEM((2, SB, D), BF16),
            dma((17,)), dma((17,)), dma((17,)), dma((17,)), dma((17,)), dma((17,)),
            dma((9,)), dma((9,)), dma((16,)), dma((16,)), dma((2,)), dma((3,)),
        ],
        compiler_params=pltpu.CompilerParams(
            collective_id=0, has_side_effects=True, vmem_limit_bytes=60 * 2**20
        ),
        cost_estimate=pl.CostEstimate(
            flops=18_000_000_000, bytes_accessed=4_000_000, transcendentals=21_000_000
        ),
    )(
        target[0], ref_slots[0], norm_gain[None, :], w_qkv.reshape(D, 3 * HD), factor, sel, w_out
    )
    return out[None]


def solution(mesh):
    placed = (
        P("view", "seq", None),
        P("view", "seq", None),
        P(),
        P(),
        P(None, None, "seq"),
        P("seq"),
        P("seq", None),
    )
    return jax.shard_map(
        local, mesh=mesh, in_specs=placed, out_specs=P("view", "seq", None), check_vma=False
    )
```

```python
import math

import jax
import jax.numpy as jnp
from jax import lax
from jax.experimental import pallas as pl
from jax.experimental.pallas import tpu as pltpu
from jax.sharding import PartitionSpec as P

HD = 128
D = 2048
LEN = 2048
TB = 128
SB = 64
RC = 1024
QB = 512
MESH = pl.DeviceIdType.MESH
F32 = jnp.float32
BF16 = jnp.bfloat16
NT = (((1,), (1,)), ((), ()))


def rows(start, size):
    return pl.ds(pl.multiple_of(start, size), size)


def normalise(x, gain):
    xf = x.astype(F32)
    scaled = xf * lax.rsqrt(jnp.mean(xf * xf, axis=-1, keepdims=True) + 1e-06)
    return (scaled * gain).astype(BF16)


class Copies:
    def __init__(self, buf, size, place, me, ring, partner, sibling, send, recv):
        self.buf, self.size, self.place = buf, size, place
        self.pos, self.side = me
        self.ring, self.partner, self.sibling = ring, partner, sibling
        self.send, self.recv = send, recv
        self.started = []

    def region(self, shift, k, half=None):
        pos = lax.rem(self.pos + shift, 4)
        side = self.side if k == 0 else 1 - self.side
        start = self.place(pos, side) * self.size
        if half is None:
            return self.buf.at[rows(start, self.size)]
        part = self.size // 2
        return self.buf.at[rows(start + half * part, part)]

    def put(self, region, device, sem):
        copy = pltpu.make_async_remote_copy(
            src_ref=region,
            dst_ref=region,
            send_sem=self.send.at[len(self.started)],
            recv_sem=self.recv.at[sem],
            device_id=device,
            device_id_type=MESH,
        )
        copy.start()
        self.started.append(copy)

    def got(self, region, sem):
        pltpu.make_async_remote_copy(
            src_ref=region,
            dst_ref=region,
            send_sem=self.send.at[0],
            recv_sem=self.recv.at[sem],
            device_id=self.partner,
            device_id_type=MESH,
        ).wait_recv()

    def close(self):
        for copy in self.started:
            copy.wait_send()


class PartnerFirst(Copies):
    def share(self, shift, k):
        self.put(self.region(shift, k), self.sibling, 9 + {0: 0, 3: 2, 1: 4, 2: 6}[shift] + k)

    def own(self):
        block = self.region(0, 0)
        self.put(block, self.partner, 0)
        self.put(block, self.ring[0], 1)
        self.put(block, self.ring[1], 3)
        self.share(0, 0)

    def pass_partner(self):
        block = self.region(0, 1)
        self.got(block, 0)
        self.put(block, self.ring[0], 2)
        self.put(block, self.ring[1], 4)
        self.share(0, 1)

    def on_below(self, k):
        self.got(self.region(3, k), 1 + k)
        self.put(self.region(3, k, 0), self.ring[0], 5 + k)
        self.share(3, k)

    def on_above(self, k):
        self.got(self.region(1, k), 3 + k)
        self.put(self.region(1, k, 1), self.ring[1], 7 + k)
        self.share(1, k)

    def on_far(self, k):
        self.got(self.region(2, k, 0), 5 + k)
        self.got(self.region(2, k, 1), 7 + k)
        self.share(2, k)

    def wait_shared(self, sibling_region, shift):
        for k in range(2):
            self.got(sibling_region(shift, k), 9 + {0: 0, 3: 2, 1: 4, 2: 6}[shift] + k)


class RingFirst(Copies):
    def share(self, shift, k):
        self.put(self.region(shift, k), self.sibling, 8 + shift * 2 + k)

    def own(self):
        block = self.region(0, 0)
        self.put(block, self.ring[0], 0)
        self.put(block, self.ring[1], 1)
        self.put(block, self.partner, 4)
        self.share(0, 0)

    def on_below(self):
        self.got(self.region(3, 0), 0)
        self.put(self.region(3, 0, 0), self.ring[0], 2)
        self.put(self.region(3, 0), self.partner, 7)
        self.share(3, 0)

    def on_above(self):
        self.got(self.region(1, 0), 1)
        self.put(self.region(1, 0, 1), self.ring[1], 3)
        self.put(self.region(1, 0), self.partner, 5)
        self.share(1, 0)

    def on_far(self):
        self.got(self.region(2, 0, 0), 2)
        self.got(self.region(2, 0, 1), 3)
        self.put(self.region(2, 0), self.partner, 6)
        self.share(2, 0)

    def on_partner(self, shift):
        self.got(self.region(shift, 1), 4 + shift)
        self.share(shift, 1)

    def wait_shared(self, sibling_region):
        for shift in range(4):
            for k in range(2):
                self.got(sibling_region(shift, k), 8 + shift * 2 + k)


class Views(Copies):
    def own(self):
        block = self.region(0, 0)
        self.put(block, self.partner, 0)
        self.put(block, self.ring[0], 1)
        self.put(block, self.ring[1], 2)

    def on_below(self):
        self.got(self.region(3, 0), 1)
        self.put(self.region(3, 0, 0), self.ring[0], 5)

    def on_above(self):
        self.got(self.region(1, 0), 2)
        self.put(self.region(1, 0, 1), self.ring[1], 6)

    def pass_partner(self):
        block = self.region(0, 1)
        self.got(block, 0)
        self.put(block, self.ring[0], 3)
        self.put(block, self.ring[1], 4)

    def on_far(self):
        self.got(self.region(2, 0, 0), 5)
        self.got(self.region(2, 0, 1), 6)
        self.put(self.region(2, 0), self.partner, 7)

    def last_below(self):
        self.got(self.region(3, 1), 3)

    def last_above(self):
        self.got(self.region(1, 1), 4)

    def last_far(self):
        self.got(self.region(2, 1), 7)


def kernel(
    owner_ref, scale_ref, x_hbm, slot_hbm, gain_ref, w_hbm, wout_hbm, out_ref,
    x_ref, slot_ref, w_ref, tok, ref_tok, wo, kv, query, acc, top, att, att_in, keep, give, moved, arrived,
    t_send, t_recv, s_send, s_recv, w_send, w_recv, r_send, r_recv, a_send, a_recv,
    m_send, m_recv, i_sem,
):
    view, seq = lax.axis_index("view"), lax.axis_index("seq")
    x, zl = view // 2, lax.rem(view, 2)
    y, zh, core = seq // 4, lax.rem(seq // 2, 2), lax.rem(seq, 2)

    def seq_of(y_, zh_, c_):
        return (y_ * 2 + zh_) * 2 + c_

    y_up, y_down = lax.rem(y + 1, 4), lax.rem(y + 3, 4)
    x_up, x_down = lax.rem(x + 1, 4), lax.rem(x + 3, 4)
    y_far, x_far = lax.rem(y + 2, 4), lax.rem(x + 2, 4)
    seq_ring = ((view, seq_of(y_up, zh, core)), (view, seq_of(y_down, zh, core)))
    seq_partner = (view, seq_of(y, 1 - zh, core))
    sibling = (view, seq_of(y, zh, 1 - core))
    view_ring = ((x_up * 2 + zl, seq), (x_down * 2 + zl, seq))
    view_partner = (x * 2 + 1 - zl, seq)
    cross = (x * 2 + 1 - zl, seq_of(y, 1 - zh, core))

    peers = []
    for dy in range(4):
        for dz in range(2):
            for dc in range(2):
                if (dy, dz, dc) != (0, 0, 0):
                    zh_ = zh if dz == 0 else 1 - zh
                    c_ = core if dc == 0 else 1 - core
                    peers.append((view, seq_of(lax.rem(y + dy, 4), zh_, c_)))
    peers += [view_partner, view_ring[0], view_ring[1], cross]
    barrier = pltpu.get_barrier_semaphore()
    for peer in peers:
        pl.semaphore_signal(barrier, inc=1, device_id=peer, device_id_type=MESH)

    load_slot = pltpu.make_async_copy(slot_hbm, slot_ref, i_sem.at[0])
    load_x = pltpu.make_async_copy(x_hbm, x_ref, i_sem.at[1])
    load_wo = pltpu.make_async_copy(wout_hbm, wo.at[rows(seq * TB, TB)], i_sem.at[2])
    load_w = [
        pltpu.make_async_copy(w_hbm.at[j], w_ref.at[:, j * HD : (j + 1) * HD], i_sem.at[3 + j])
        for j in range(3)
    ]
    for copy in [load_slot, load_x] + load_w + [load_wo]:
        copy.start()

    def seq_place(y_, zh_):
        return seq_of(y_, zh_, core)

    me = (y, zh)
    g_t = PartnerFirst(tok, TB, seq_place, me, seq_ring, seq_partner, sibling, t_send, t_recv)
    g_s = RingFirst(ref_tok, SB, seq_place, me, seq_ring, seq_partner, sibling, s_send, s_recv)
    g_w = PartnerFirst(wo, TB, seq_place, me, seq_ring, cross, sibling, w_send, w_recv)
    g_r = Views(
        kv, RC, lambda x_, zl_: x_ * 2 + zl_, (x, zl), view_ring, view_partner, None, r_send, r_recv
    )

    def of_sibling(buf, size):
        def region(shift, k):
            zh_ = zh if k == 0 else 1 - zh
            return buf.at[rows(seq_of(lax.rem(y + shift, 4), zh_, 1 - core) * size, size)]

        return region

    slots = [owner_ref[i] for i in range(4)]
    low, high = jnp.int32(99), jnp.int32(-1)
    for slot in slots:
        inner = jnp.logical_and(slot > 0, slot < 7)
        low = jnp.minimum(low, jnp.where(inner, slot, 99))
        high = jnp.maximum(high, jnp.where(inner, slot, -1))
    give_even = jnp.where(
        x == 0, 0, jnp.where(x == 1, (high == 2).astype(jnp.int32), jnp.where(x == 2, (low == 4).astype(jnp.int32), 1))
    )
    for_low = jnp.where(low == 1, 2, jnp.where(low == 2, 0, jnp.where(low == 3, 1, 3)))
    for_high = jnp.where(high == 6, 3, jnp.where(high == 4, 0, jnp.where(high == 5, 1, 2)))
    final = jnp.where(x == 0, 0, jnp.where(x == 1, for_low, jnp.where(x == 2, for_high, 1)))

    gain = gain_ref[...]
    load_slot.wait()
    give[...] = normalise(slot_ref[rows((1 - zl) * SB, SB), :], gain)
    pl.semaphore_wait(barrier, len(peers))
    part = SB // 2
    parts = [rows(i * part, part) for i in range(2)]

    def swap(i, side):
        return pltpu.make_async_remote_copy(
            src_ref=give.at[parts[i]], dst_ref=keep.at[side, parts[i]],
            send_sem=m_send.at[i], recv_sem=m_recv.at[i],
            device_id=view_partner, device_id_type=MESH,
        )

    half = x // 2

    def move(i, side):
        return pltpu.make_async_remote_copy(
            src_ref=moved.at[parts[i]], dst_ref=arrived.at[side, parts[i]],
            send_sem=m_send.at[2 + i], recv_sem=m_recv.at[2 + 2 * side + i],
            device_id=((x + 1 - 2 * half) * 2 + zl, seq), device_id_type=MESH,
        )

    for i in range(2):
        swap(i, zl).start()
    load_x.wait()
    tok[rows(seq * TB, TB), :] = normalise(x_ref[...], gain)
    g_t.own()
    keep[zl] = normalise(slot_ref[rows(zl * SB, SB), :], gain)
    for i in range(2):
        swap(i, 1 - zl).wait_recv()
        moved[parts[i], :] = jnp.where(
            give_even == 1, keep[0, parts[i], :].astype(F32), keep[1, parts[i], :].astype(F32)
        ).astype(BF16)
        move(i, half).start()
    mine = rows(seq * SB, SB)
    middle = jnp.logical_or(x == 1, x == 2)

    @pl.when(jnp.logical_not(middle))
    def _():
        ref_tok[mine, :] = jnp.where(final == 0, keep[0].astype(F32), keep[1].astype(F32)).astype(BF16)

    @pl.when(middle)
    def _():
        for i in range(2):
            for side in range(2):
                move(i, side).wait_recv()
        near = jnp.where(final == 0, keep[0].astype(F32), keep[1].astype(F32))
        far = jnp.where(final == 2, arrived[0].astype(F32), arrived[1].astype(F32))
        ref_tok[mine, :] = jnp.where(final < 2, near, far).astype(BF16)

    factor = scale_ref[0] * (HD ** (-0.5) * math.log2(math.e))

    def project(y_):
        at = rows(y_ * QB, QB)
        qkv = jnp.dot(tok[at, :], w_ref[...], preferred_element_type=F32).astype(BF16)
        kv[rows(4 * LEN + y_ * QB, QB), :] = qkv[:, HD:]
        scaled = qkv[:, :HD].astype(F32) * factor
        high_part = scaled.astype(BF16)
        low_part = (scaled - high_part.astype(F32)).astype(BF16)
        query[at, :] = jnp.concatenate([high_part, low_part], axis=1)

    tok_shared = of_sibling(tok, TB)
    g_s.own()
    g_t.pass_partner()
    g_t.on_below(0)
    g_t.on_above(0)
    for copy in load_w:
        copy.wait()
    g_s.on_below()
    g_s.on_above()
    g_s.on_partner(0)
    g_t.wait_shared(tok_shared, 0)
    project(y)
    g_t.on_below(1)
    g_t.on_above(1)
    g_s.on_far()
    g_s.on_partner(1)
    g_s.on_partner(3)
    g_s.on_partner(2)
    g_s.wait_shared(of_sibling(ref_tok, SB))

    def ref_project(i, _):
        own_kv = jnp.dot(ref_tok[rows(i * QB, QB), :], w_ref[:, HD:], preferred_element_type=F32)
        kv[rows(view * RC + i * QB, QB), :] = own_kv.astype(BF16)
        return 0

    lax.fori_loop(0, RC // QB, ref_project, 0)
    g_r.own()
    g_t.wait_shared(tok_shared, 3)
    project(y_down)
    g_t.wait_shared(tok_shared, 1)
    project(y_up)
    g_t.on_far(0)
    g_t.on_far(1)
    load_wo.wait()
    g_w.own()
    g_t.wait_shared(tok_shared, 2)
    project(y_far)

    def attend(starts, size, first=False, last=None):
        count = size * len(starts)
        pieces = [kv[rows(start, size), :] for start in starts]
        both = pieces[0] if len(pieces) == 1 else jnp.concatenate(pieces, axis=0)
        keys = jnp.concatenate([both[:, :HD], both[:, :HD]], axis=1)
        values = jnp.concatenate([both[:, HD:], jnp.ones((count, HD), BF16)], axis=1)

        def block(t):
            return rows(lax.rem(y + 1 + t, 4) * QB, QB)

        def score(t):
            return lax.dot_general(query[block(t), :], keys, NT, preferred_element_type=F32)

        ahead = score(0)
        for t in range(LEN // QB):
            scores = ahead
            if t + 1 < LEN // QB:
                ahead = score(t + 1)
            q = block(t)
            peak = jnp.max(scores, axis=1, keepdims=True)
            if first:
                new = jnp.broadcast_to(peak, (QB, HD))
            else:
                old = top[q, :]
                new = jnp.maximum(old, peak)
            weights = jnp.exp2(scores - jnp.tile(new, (1, count // HD))).astype(BF16)
            total = jnp.dot(weights, values, preferred_element_type=F32)
            if not first:
                total += acc[q, :] * jnp.tile(jnp.exp2(old - new), (1, 2))
            if last:
                att[q, :] = (total[:, :HD] / total[:, HD:]).astype(BF16)
                last(t)
            else:
                top[q, :] = new
                acc[q, :] = total

    sent = []

    def hand_out(t):
        y_ = lax.rem(y + 1 + t, 4)
        for combo in range(4):
            zh_ = zh if combo < 2 else 1 - zh
            c_ = core if combo % 2 == 0 else 1 - core
            to = seq_of(y_, zh_, c_)
            if t == 3 and combo == 0:
                att_in[:, rows(seq * HD, HD)] = att[rows(seq * TB, TB), :]
                continue
            copy = pltpu.make_async_remote_copy(
                src_ref=att.at[rows(to * TB, TB)],
                dst_ref=att_in.at[:, rows(seq * HD, HD)],
                send_sem=a_send.at[t * 4 + combo],
                recv_sem=a_recv.at[t * 4 + combo],
                device_id=(view, to),
                device_id_type=MESH,
            )
            copy.start()
            sent.append(copy)

    def group(x_, zl_):
        return (x_ * 2 + zl_) * RC

    attend([4 * LEN], LEN, first=True)
    g_r.on_below()
    g_r.on_above()
    g_r.pass_partner()
    g_w.pass_partner()
    attend([group(x, zl)], RC)
    g_w.on_below(0)
    g_w.on_above(0)
    attend([group(x, 1 - zl)], RC)
    g_r.on_far()
    attend([group(x_down, zl)], RC)
    attend([group(x_up, zl)], RC)
    g_w.on_below(1)
    g_w.on_above(1)
    attend([group(x_far, zl)], RC)
    g_r.last_below()
    attend([group(x_down, 1 - zl)], RC)
    g_w.on_far(0)
    g_w.on_far(1)
    g_r.last_above()
    g_r.last_far()
    attend([group(x_up, 1 - zl), group(x_far, 1 - zl)], RC, last=hand_out)

    for shift in range(4):
        g_w.wait_shared(of_sibling(wo, TB), shift)
    for t in range(4):
        for combo in range(4):
            if t == 3 and combo == 0:
                continue
            y_ = lax.rem(y + 3 - t, 4)
            zh_ = zh if combo < 2 else 1 - zh
            c_ = core if combo % 2 == 0 else 1 - core
            pltpu.make_async_remote_copy(
                src_ref=att.at[rows(0, TB)],
                dst_ref=att_in.at[:, rows(seq_of(y_, zh_, c_) * HD, HD)],
                send_sem=a_send.at[0],
                recv_sem=a_recv.at[t * 4 + combo],
                device_id=sibling,
                device_id_type=MESH,
            ).wait_recv()

    def output(i, _):
        at = rows(i * QB, QB)
        out_ref[:, at] = jnp.dot(att_in[...], wo[:, at], preferred_element_type=F32).astype(BF16)
        return 0

    lax.fori_loop(0, D // QB, output, 0)
    for i in range(2):
        swap(i, zl).wait_send()
        move(i, half).wait_send()
    for gather in (g_t, g_s, g_w, g_r):
        gather.close()
    for copy in sent:
        copy.wait_send()


def local(target, ref_slots, owners, norm_gain, w_qkv, head_scale, w_out):
    vmem = pl.BlockSpec(memory_space=pltpu.VMEM)
    smem = pl.BlockSpec(memory_space=pltpu.SMEM)
    hbm = pl.BlockSpec(memory_space=pl.ANY)
    dma = pltpu.SemaphoreType.DMA
    out = pl.pallas_call(
        kernel,
        out_shape=jax.ShapeDtypeStruct((TB, D), BF16),
        in_specs=[smem, smem, hbm, hbm, vmem, hbm, hbm],
        out_specs=vmem,
        scratch_shapes=[
            pltpu.VMEM((TB, D), BF16),
            pltpu.VMEM((TB, D), BF16),
            pltpu.VMEM((D, 3 * HD), BF16),
            pltpu.VMEM((LEN, D), BF16),
            pltpu.VMEM((RC, D), BF16),
            pltpu.VMEM((D, D), BF16),
            pltpu.VMEM((5 * LEN, 2 * HD), BF16),
            pltpu.VMEM((LEN, 2 * HD), BF16),
            pltpu.VMEM((LEN, 2 * HD), F32),
            pltpu.VMEM((LEN, HD), F32),
            pltpu.VMEM((LEN, HD), BF16),
            pltpu.VMEM((TB, D), BF16),
            pltpu.VMEM((2, SB, D), BF16),
            pltpu.VMEM((SB, D), BF16),
            pltpu.VMEM((SB, D), BF16),
            pltpu.VMEM((2, SB, D), BF16),
            dma((17,)), dma((17,)), dma((16,)), dma((16,)), dma((17,)), dma((17,)),
            dma((8,)), dma((8,)), dma((16,)), dma((16,)), dma((4,)), dma((6,)), dma((6,)),
        ],
        compiler_params=pltpu.CompilerParams(
            collective_id=0, has_side_effects=True, vmem_limit_bytes=60 * 2**20
        ),
        cost_estimate=pl.CostEstimate(
            flops=18_000_000_000, bytes_accessed=4_000_000, transcendentals=21_000_000
        ),
    )(
        owners, head_scale, target[0], ref_slots[0], norm_gain[None, :],
        jnp.transpose(w_qkv, (1, 0, 2)), w_out,
    )
    return out[None]


def solution(mesh):
    placed = (
        P("view", "seq", None),
        P("view", "seq", None),
        P(),
        P(),
        P(None, None, "seq"),
        P("seq"),
        P("seq", None),
    )
    return jax.shard_map(
        local, mesh=mesh, in_specs=placed, out_specs=P("view", "seq", None), check_vma=False
    )
```

```python
import math

import jax
import jax.numpy as jnp
from jax import lax
from jax.experimental import pallas as pl
from jax.experimental.pallas import tpu as pltpu
from jax.sharding import PartitionSpec as P

HD = 128
D = 2048
LEN = 2048
TB = 128
SB = 64
RC = 1024
QB = 512
MESH = pl.DeviceIdType.MESH
F32 = jnp.float32
BF16 = jnp.bfloat16
NT = (((1,), (1,)), ((), ()))


def rows(start, size):
    return pl.ds(pl.multiple_of(start, size), size)


def normalise(x, gain):
    xf = x.astype(F32)
    scaled = xf * lax.rsqrt(jnp.mean(xf * xf, axis=-1, keepdims=True) + 1e-06)
    return (scaled * gain).astype(BF16)


class Copies:
    def __init__(self, buf, size, place, me, ring, partner, sibling, send, recv):
        self.buf, self.size, self.place = buf, size, place
        self.pos, self.side = me
        self.ring, self.partner, self.sibling = ring, partner, sibling
        self.send, self.recv = send, recv
        self.started = []

    def region(self, shift, k, half=None):
        pos = lax.rem(self.pos + shift, 4)
        side = self.side if k == 0 else 1 - self.side
        start = self.place(pos, side)
        if half is None:
            return self.buf.at[rows(start, self.size)]
        part = self.size // 2
        return self.buf.at[rows(start + half * part, part)]

    def put(self, region, device, sem):
        copy = pltpu.make_async_remote_copy(
            src_ref=region,
            dst_ref=region,
            send_sem=self.send.at[len(self.started)],
            recv_sem=self.recv.at[sem],
            device_id=device,
            device_id_type=MESH,
        )
        copy.start()
        self.started.append(copy)

    def got(self, region, sem):
        pltpu.make_async_remote_copy(
            src_ref=region,
            dst_ref=region,
            send_sem=self.send.at[0],
            recv_sem=self.recv.at[sem],
            device_id=self.partner,
            device_id_type=MESH,
        ).wait_recv()

    def close(self):
        for copy in self.started:
            copy.wait_send()


class PartnerFirst(Copies):
    def share(self, shift, k):
        self.put(self.region(shift, k), self.sibling, 9 + {0: 0, 3: 2, 1: 4, 2: 6}[shift] + k)

    def own(self):
        block = self.region(0, 0)
        self.put(block, self.partner, 0)
        self.put(block, self.ring[0], 1)
        self.put(block, self.ring[1], 3)
        self.share(0, 0)

    def pass_partner(self):
        block = self.region(0, 1)
        self.got(block, 0)
        self.put(block, self.ring[0], 2)
        self.put(block, self.ring[1], 4)
        self.share(0, 1)

    def on_below(self, k):
        self.got(self.region(3, k), 1 + k)
        self.put(self.region(3, k, 0), self.ring[0], 5 + k)
        self.share(3, k)

    def on_above(self, k):
        self.got(self.region(1, k), 3 + k)
        self.put(self.region(1, k, 1), self.ring[1], 7 + k)
        self.share(1, k)

    def on_far(self, k):
        self.got(self.region(2, k, 0), 5 + k)
        self.got(self.region(2, k, 1), 7 + k)
        self.share(2, k)

    def wait_shared(self, sibling_region, shift):
        for k in range(2):
            self.got(sibling_region(shift, k), 9 + {0: 0, 3: 2, 1: 4, 2: 6}[shift] + k)


class FarAcross(PartnerFirst):
    def on_below(self, k):
        if k == 0:
            super().on_below(k)
        else:
            self.got(self.region(3, k), 1 + k)
            self.share(3, k)

    def on_above(self, k):
        if k == 0:
            super().on_above(k)
        else:
            self.got(self.region(1, k), 3 + k)
            self.share(1, k)

    def on_far(self, k):
        if k == 0:
            super().on_far(k)
            self.put(self.region(2, 0), self.partner, 6)
        else:
            self.got(self.region(2, 1), 6)
            self.share(2, 1)


class RingFirst(Copies):
    def share(self, shift, k):
        self.put(self.region(shift, k), self.sibling, 8 + shift * 2 + k)

    def own(self):
        block = self.region(0, 0)
        self.put(block, self.ring[0], 0)
        self.put(block, self.ring[1], 1)
        self.put(block, self.partner, 4)
        self.share(0, 0)

    def on_below(self):
        self.got(self.region(3, 0), 0)
        self.put(self.region(3, 0, 0), self.ring[0], 2)
        self.put(self.region(3, 0), self.partner, 7)
        self.share(3, 0)

    def on_above(self):
        self.got(self.region(1, 0), 1)
        self.put(self.region(1, 0, 1), self.ring[1], 3)
        self.put(self.region(1, 0), self.partner, 5)
        self.share(1, 0)

    def on_far(self):
        self.got(self.region(2, 0, 0), 2)
        self.got(self.region(2, 0, 1), 3)
        self.put(self.region(2, 0), self.partner, 6)
        self.share(2, 0)

    def on_partner(self, shift):
        self.got(self.region(shift, 1), 4 + shift)
        self.share(shift, 1)

    def wait_shared(self, sibling_region):
        for shift in range(4):
            for k in range(2):
                self.got(sibling_region(shift, k), 8 + shift * 2 + k)


class Views(Copies):
    def own(self):
        block = self.region(0, 0)
        self.put(block, self.partner, 0)
        self.put(block, self.ring[0], 1)
        self.put(block, self.ring[1], 2)

    def on_below(self):
        self.got(self.region(3, 0), 1)
        self.put(self.region(3, 0, 0), self.ring[0], 5)

    def on_above(self):
        self.got(self.region(1, 0), 2)
        self.put(self.region(1, 0, 1), self.ring[1], 6)

    def pass_partner(self):
        block = self.region(0, 1)
        self.got(block, 0)
        self.put(block, self.ring[0], 3)
        self.put(block, self.ring[1], 4)

    def on_far(self):
        self.got(self.region(2, 0, 0), 5)
        self.got(self.region(2, 0, 1), 6)
        self.put(self.region(2, 0), self.partner, 7)

    def last_below(self):
        self.got(self.region(3, 1), 3)

    def last_above(self):
        self.got(self.region(1, 1), 4)

    def last_far(self):
        self.got(self.region(2, 1), 7)


def kernel(
    owner_ref, scale_ref, x_hbm, slot_hbm, gain_ref, w_hbm, wout_hbm, out_ref,
    x_ref, slot_ref, w_ref, tok, ref_tok, wo, kv, query, acc, top, att, att_in, keep, give, moved, arrived,
    t_send, t_recv, s_send, s_recv, s2_send, s2_recv, w_send, w_recv, r_send, r_recv, a_send, a_recv,
    m_send, m_recv, i_sem,
):
    view, seq = lax.axis_index("view"), lax.axis_index("seq")
    x, zl = view // 2, lax.rem(view, 2)
    y, zh, core = seq // 4, lax.rem(seq // 2, 2), lax.rem(seq, 2)

    def seq_of(y_, zh_, c_):
        return (y_ * 2 + zh_) * 2 + c_

    y_up, y_down = lax.rem(y + 1, 4), lax.rem(y + 3, 4)
    x_up, x_down = lax.rem(x + 1, 4), lax.rem(x + 3, 4)
    y_far, x_far = lax.rem(y + 2, 4), lax.rem(x + 2, 4)
    seq_ring = ((view, seq_of(y_up, zh, core)), (view, seq_of(y_down, zh, core)))
    seq_partner = (view, seq_of(y, 1 - zh, core))
    sibling = (view, seq_of(y, zh, 1 - core))
    view_ring = ((x_up * 2 + zl, seq), (x_down * 2 + zl, seq))
    view_partner = (x * 2 + 1 - zl, seq)
    cross = (x * 2 + 1 - zl, seq_of(y, 1 - zh, core))

    peers = []
    for dy in range(4):
        for dz in range(2):
            for dc in range(2):
                if (dy, dz, dc) != (0, 0, 0):
                    zh_ = zh if dz == 0 else 1 - zh
                    c_ = core if dc == 0 else 1 - core
                    peers.append((view, seq_of(lax.rem(y + dy, 4), zh_, c_)))
    peers += [view_partner, view_ring[0], view_ring[1], cross]
    barrier = pltpu.get_barrier_semaphore()
    for peer in peers:
        pl.semaphore_signal(barrier, inc=1, device_id=peer, device_id_type=MESH)

    load_slot = pltpu.make_async_copy(slot_hbm, slot_ref, i_sem.at[0])
    load_x = pltpu.make_async_copy(x_hbm, x_ref, i_sem.at[1])
    load_wo = pltpu.make_async_copy(wout_hbm, wo.at[rows(seq * TB, TB)], i_sem.at[2])
    load_w = [
        pltpu.make_async_copy(w_hbm.at[j], w_ref.at[:, j * HD : (j + 1) * HD], i_sem.at[3 + j])
        for j in range(3)
    ]
    for copy in [load_slot, load_x, load_wo] + load_w:
        copy.start()

    def seq_place(stride, base=0):
        return lambda y_, zh_: seq_of(y_, zh_, core) * stride + base

    me = (y, zh)
    part = SB // 2
    g_t = PartnerFirst(tok, TB, seq_place(TB), me, seq_ring, seq_partner, sibling, t_send, t_recv)
    g_w = FarAcross(wo, TB, seq_place(TB), me, seq_ring, cross, sibling, w_send, w_recv)
    s_ring = RingFirst(ref_tok, part, seq_place(SB), me, seq_ring, seq_partner, sibling, s_send, s_recv)
    s_part = PartnerFirst(
        ref_tok, part, seq_place(SB, part), me, seq_ring, seq_partner, sibling, s2_send, s2_recv
    )
    g_r = Views(
        kv, RC, lambda x_, zl_: (x_ * 2 + zl_) * RC, (x, zl), view_ring, view_partner, None, r_send, r_recv
    )

    def of_sibling(buf, size, stride, base=0):
        def region(shift, k):
            zh_ = zh if k == 0 else 1 - zh
            start = seq_of(lax.rem(y + shift, 4), zh_, 1 - core) * stride + base
            return buf.at[rows(start, size)]

        return region

    slots = [owner_ref[i] for i in range(4)]
    low, high = jnp.int32(99), jnp.int32(-1)
    for slot in slots:
        inner = jnp.logical_and(slot > 0, slot < 7)
        low = jnp.minimum(low, jnp.where(inner, slot, 99))
        high = jnp.maximum(high, jnp.where(inner, slot, -1))
    give_even = jnp.where(
        x == 0, 0, jnp.where(x == 1, (high == 2).astype(jnp.int32), jnp.where(x == 2, (low == 4).astype(jnp.int32), 1))
    )
    for_low = jnp.where(low == 1, 2, jnp.where(low == 2, 0, jnp.where(low == 3, 1, 3)))
    for_high = jnp.where(high == 6, 3, jnp.where(high == 4, 0, jnp.where(high == 5, 1, 2)))
    final = jnp.where(x == 0, 0, jnp.where(x == 1, for_low, jnp.where(x == 2, for_high, 1)))

    gain = gain_ref[...]
    load_slot.wait()
    give[...] = normalise(slot_ref[rows((1 - zl) * SB, SB), :], gain)
    pl.semaphore_wait(barrier, len(peers))
    parts = [rows(i * part, part) for i in range(2)]

    def swap(i, side):
        return pltpu.make_async_remote_copy(
            src_ref=give.at[parts[i]], dst_ref=keep.at[side, parts[i]],
            send_sem=m_send.at[i], recv_sem=m_recv.at[i],
            device_id=view_partner, device_id_type=MESH,
        )

    half = x // 2

    def move(i, side):
        return pltpu.make_async_remote_copy(
            src_ref=moved.at[parts[i]], dst_ref=arrived.at[side, parts[i]],
            send_sem=m_send.at[2 + i], recv_sem=m_recv.at[2 + 2 * side + i],
            device_id=((x + 1 - 2 * half) * 2 + zl, seq), device_id_type=MESH,
        )

    for i in range(2):
        swap(i, zl).start()
    load_x.wait()
    tok[rows(seq * TB, TB), :] = normalise(x_ref[...], gain)
    g_t.own()
    keep[zl] = normalise(slot_ref[rows(zl * SB, SB), :], gain)
    for i in range(2):
        swap(i, 1 - zl).wait_recv()
        moved[parts[i], :] = jnp.where(
            give_even == 1, keep[0, parts[i], :].astype(F32), keep[1, parts[i], :].astype(F32)
        ).astype(BF16)
        move(i, half).start()
    mine = rows(seq * SB, SB)
    middle = jnp.logical_or(x == 1, x == 2)

    @pl.when(jnp.logical_not(middle))
    def _():
        ref_tok[mine, :] = jnp.where(final == 0, keep[0].astype(F32), keep[1].astype(F32)).astype(BF16)

    @pl.when(middle)
    def _():
        for i in range(2):
            for side in range(2):
                move(i, side).wait_recv()
        near = jnp.where(final == 0, keep[0].astype(F32), keep[1].astype(F32))
        far = jnp.where(final == 2, arrived[0].astype(F32), arrived[1].astype(F32))
        ref_tok[mine, :] = jnp.where(final < 2, near, far).astype(BF16)

    factor = scale_ref[0] * (HD ** (-0.5) * math.log2(math.e))

    def project(y_):
        at = rows(y_ * QB, QB)
        qkv = jnp.dot(tok[at, :], w_ref[...], preferred_element_type=F32).astype(BF16)
        kv[rows(4 * LEN + y_ * QB, QB), :] = qkv[:, HD:]
        scaled = qkv[:, :HD].astype(F32) * factor
        high_part = scaled.astype(BF16)
        low_part = (scaled - high_part.astype(F32)).astype(BF16)
        query[at, :] = jnp.concatenate([high_part, low_part], axis=1)

    tok_shared = of_sibling(tok, TB, TB)
    s_ring.own()
    s_part.own()
    g_t.on_below(0)
    g_t.on_above(0)
    s_part.pass_partner()
    s_ring.on_below()
    s_ring.on_above()
    s_part.on_below(0)
    s_part.on_above(0)
    s_ring.on_partner(0)
    s_ring.on_far()
    s_part.on_below(1)
    s_part.on_above(1)
    g_t.pass_partner()
    for copy in load_w:
        copy.wait()
    s_ring.on_partner(1)
    s_ring.on_partner(3)
    s_part.on_far(0)
    s_part.on_far(1)
    s_ring.on_partner(2)
    s_ring.wait_shared(of_sibling(ref_tok, part, SB))
    for shift in range(4):
        s_part.wait_shared(of_sibling(ref_tok, part, SB, part), shift)

    def ref_project(i, _):
        own_kv = jnp.dot(ref_tok[rows(i * QB, QB), :], w_ref[:, HD:], preferred_element_type=F32)
        kv[rows(view * RC + i * QB, QB), :] = own_kv.astype(BF16)
        return 0

    lax.fori_loop(0, RC // QB, ref_project, 0)
    g_r.own()

    begun = set()

    def attend(items, last=None):
        loaded = {}

        def block(t):
            return rows(lax.rem(y + 1 + t, 4) * QB, QB)

        def score(item):
            name, start, size, t = item
            if name not in loaded:
                both = kv[rows(start, size), :]
                loaded[name] = (
                    jnp.concatenate([both[:, :HD], both[:, :HD]], axis=1),
                    jnp.concatenate([both[:, HD:], jnp.ones((size, HD), BF16)], axis=1),
                )
            return lax.dot_general(query[block(t), :], loaded[name][0], NT, preferred_element_type=F32)

        ahead = score(items[0])
        for index, (name, start, size, t) in enumerate(items):
            scores = ahead
            if index + 1 < len(items):
                ahead = score(items[index + 1])
            q = block(t)
            first = t not in begun
            begun.add(t)
            peak = jnp.max(scores, axis=1, keepdims=True)
            if first:
                new = jnp.broadcast_to(peak, (QB, HD))
            else:
                old = top[q, :]
                new = jnp.maximum(old, peak)
            weights = jnp.exp2(scores - jnp.tile(new, (1, size // HD))).astype(BF16)
            total = jnp.dot(weights, loaded[name][1], preferred_element_type=F32)
            if not first:
                total += acc[q, :] * jnp.tile(jnp.exp2(old - new), (1, 2))
            if last:
                att[q, :] = (total[:, :HD] / total[:, HD:]).astype(BF16)
                last(t)
            else:
                top[q, :] = new
                acc[q, :] = total

    sent = []

    def hand_out(t):
        y_ = lax.rem(y + 1 + t, 4)
        for combo in range(4):
            zh_ = zh if combo < 2 else 1 - zh
            c_ = core if combo % 2 == 0 else 1 - core
            to = seq_of(y_, zh_, c_)
            if t == 3 and combo == 0:
                att_in[:, rows(seq * HD, HD)] = att[rows(seq * TB, TB), :]
                continue
            copy = pltpu.make_async_remote_copy(
                src_ref=att.at[rows(to * TB, TB)],
                dst_ref=att_in.at[:, rows(seq * HD, HD)],
                send_sem=a_send.at[t * 4 + combo],
                recv_sem=a_recv.at[t * 4 + combo],
                device_id=(view, to),
                device_id_type=MESH,
            )
            copy.start()
            sent.append(copy)

    def group(x_, zl_):
        return (x_ * 2 + zl_) * RC

    def pair(x_, ts=range(4)):
        return [("pair", group(x_, 0), LEN, t) for t in ts]

    near = (3, 2, 0)
    g_t.wait_shared(tok_shared, 0)
    project(y)
    g_t.on_below(1)
    g_t.on_above(1)
    g_t.on_far(0)
    g_t.wait_shared(tok_shared, 3)
    project(y_down)
    g_t.wait_shared(tok_shared, 1)
    project(y_up)
    attend([("own", group(x, zl), RC, t) for t in near])
    g_r.on_below()
    g_r.on_above()
    g_r.pass_partner()
    g_t.on_far(1)
    load_wo.wait()
    g_w.own()
    attend([("partner", group(x, 1 - zl), RC, t) for t in near])
    g_r.on_far()
    g_t.wait_shared(tok_shared, 2)
    project(y_far)
    attend(pair(x, (1,)) + [("view", 4 * LEN, LEN, t) for t in range(4)])
    g_w.on_below(0)
    g_w.on_above(0)
    g_w.pass_partner()
    g_r.last_below()
    attend(pair(x_down))
    g_r.last_above()
    g_w.on_far(0)
    attend(pair(x_up))
    g_r.last_far()
    attend(pair(x_far), last=hand_out)

    g_w.on_below(1)
    g_w.on_above(1)
    g_w.on_far(1)
    for shift in range(4):
        g_w.wait_shared(of_sibling(wo, TB, TB), shift)
    for t in range(4):
        for combo in range(4):
            if t == 3 and combo == 0:
                continue
            y_ = lax.rem(y + 3 - t, 4)
            zh_ = zh if combo < 2 else 1 - zh
            c_ = core if combo % 2 == 0 else 1 - core
            pltpu.make_async_remote_copy(
                src_ref=att.at[rows(0, TB)],
                dst_ref=att_in.at[:, rows(seq_of(y_, zh_, c_) * HD, HD)],
                send_sem=a_send.at[0],
                recv_sem=a_recv.at[t * 4 + combo],
                device_id=sibling,
                device_id_type=MESH,
            ).wait_recv()

    def output(i, _):
        at = rows(i * QB, QB)
        out_ref[:, at] = jnp.dot(att_in[...], wo[:, at], preferred_element_type=F32).astype(BF16)
        return 0

    lax.fori_loop(0, D // QB, output, 0)
    for i in range(2):
        swap(i, zl).wait_send()
        move(i, half).wait_send()
    for gather in (g_t, s_ring, s_part, g_w, g_r):
        gather.close()
    for copy in sent:
        copy.wait_send()


def local(target, ref_slots, owners, norm_gain, w_qkv, head_scale, w_out):
    vmem = pl.BlockSpec(memory_space=pltpu.VMEM)
    smem = pl.BlockSpec(memory_space=pltpu.SMEM)
    hbm = pl.BlockSpec(memory_space=pl.ANY)
    dma = pltpu.SemaphoreType.DMA
    out = pl.pallas_call(
        kernel,
        out_shape=jax.ShapeDtypeStruct((TB, D), BF16),
        in_specs=[smem, smem, hbm, hbm, vmem, hbm, hbm],
        out_specs=vmem,
        scratch_shapes=[
            pltpu.VMEM((TB, D), BF16),
            pltpu.VMEM((TB, D), BF16),
            pltpu.VMEM((D, 3 * HD), BF16),
            pltpu.VMEM((LEN, D), BF16),
            pltpu.VMEM((RC, D), BF16),
            pltpu.VMEM((D, D), BF16),
            pltpu.VMEM((5 * LEN, 2 * HD), BF16),
            pltpu.VMEM((LEN, 2 * HD), BF16),
            pltpu.VMEM((LEN, 2 * HD), F32),
            pltpu.VMEM((LEN, HD), F32),
            pltpu.VMEM((LEN, HD), BF16),
            pltpu.VMEM((TB, D), BF16),
            pltpu.VMEM((2, SB, D), BF16),
            pltpu.VMEM((SB, D), BF16),
            pltpu.VMEM((SB, D), BF16),
            pltpu.VMEM((2, SB, D), BF16),
            dma((17,)), dma((17,)), dma((16,)), dma((16,)), dma((17,)), dma((17,)), dma((17,)), dma((17,)),
            dma((8,)), dma((8,)), dma((16,)), dma((16,)), dma((4,)), dma((6,)), dma((6,)),
        ],
        compiler_params=pltpu.CompilerParams(
            collective_id=0, has_side_effects=True, vmem_limit_bytes=60 * 2**20
        ),
        cost_estimate=pl.CostEstimate(
            flops=18_000_000_000, bytes_accessed=4_000_000, transcendentals=21_000_000
        ),
    )(
        owners, head_scale, target[0], ref_slots[0], norm_gain[None, :],
        jnp.transpose(w_qkv, (1, 0, 2)), w_out,
    )
    return out[None]


def solution(mesh):
    placed = (
        P("view", "seq", None),
        P("view", "seq", None),
        P(),
        P(),
        P(None, None, "seq"),
        P("seq"),
        P("seq", None),
    )
    return jax.shard_map(
        local, mesh=mesh, in_specs=placed, out_specs=P("view", "seq", None), check_vma=False
    )
```

```python
import math

import jax
import jax.numpy as jnp
from jax import lax
from jax.experimental import pallas as pl
from jax.experimental.pallas import tpu as pltpu
from jax.sharding import PartitionSpec as P

HD = 128
D = 2048
LEN = 2048
TB = 128
SB = 64
RC = 1024
QB = 512
MESH = pl.DeviceIdType.MESH
F32 = jnp.float32
BF16 = jnp.bfloat16
NT = (((1,), (1,)), ((), ()))


def rows(start, size):
    return pl.ds(pl.multiple_of(start, size), size)


def normalise(x, gain):
    xf = x.astype(F32)
    scaled = xf * lax.rsqrt(jnp.mean(xf * xf, axis=-1, keepdims=True) + 1e-06)
    return (scaled * gain).astype(BF16)


class Copies:
    def __init__(self, buf, size, place, me, ring, partner, sibling, send, recv):
        self.buf, self.size, self.place = buf, size, place
        self.pos, self.side = me
        self.ring, self.partner, self.sibling = ring, partner, sibling
        self.send, self.recv = send, recv
        self.started = []

    def region(self, shift, k, half=None):
        pos = lax.rem(self.pos + shift, 4)
        side = self.side if k == 0 else 1 - self.side
        start = self.place(pos, side)
        if half is None:
            return self.buf.at[rows(start, self.size)]
        part = self.size // 2
        return self.buf.at[rows(start + half * part, part)]

    def put(self, region, device, sem):
        copy = pltpu.make_async_remote_copy(
            src_ref=region,
            dst_ref=region,
            send_sem=self.send.at[len(self.started)],
            recv_sem=self.recv.at[sem],
            device_id=device,
            device_id_type=MESH,
        )
        copy.start()
        self.started.append(copy)

    def got(self, region, sem):
        pltpu.make_async_remote_copy(
            src_ref=region,
            dst_ref=region,
            send_sem=self.send.at[0],
            recv_sem=self.recv.at[sem],
            device_id=self.partner,
            device_id_type=MESH,
        ).wait_recv()

    def close(self):
        for copy in self.started:
            copy.wait_send()


class PartnerFirst(Copies):
    def share(self, shift, k):
        self.put(self.region(shift, k), self.sibling, 9 + {0: 0, 3: 2, 1: 4, 2: 6}[shift] + k)

    def own(self):
        block = self.region(0, 0)
        self.put(block, self.partner, 0)
        self.put(block, self.ring[0], 1)
        self.put(block, self.ring[1], 3)
        self.share(0, 0)

    def pass_partner(self):
        block = self.region(0, 1)
        self.got(block, 0)
        self.put(block, self.ring[0], 2)
        self.put(block, self.ring[1], 4)
        self.share(0, 1)

    def on_below(self, k):
        self.got(self.region(3, k), 1 + k)
        self.put(self.region(3, k, 0), self.ring[0], 5 + k)
        self.share(3, k)

    def on_above(self, k):
        self.got(self.region(1, k), 3 + k)
        self.put(self.region(1, k, 1), self.ring[1], 7 + k)
        self.share(1, k)

    def on_far(self, k):
        self.got(self.region(2, k, 0), 5 + k)
        self.got(self.region(2, k, 1), 7 + k)
        self.share(2, k)

    def wait_shared(self, sibling_region, shift):
        for k in range(2):
            self.got(sibling_region(shift, k), 9 + {0: 0, 3: 2, 1: 4, 2: 6}[shift] + k)


class FarAcross(PartnerFirst):
    def on_below(self, k):
        if k == 0:
            super().on_below(k)
        else:
            self.got(self.region(3, k), 1 + k)
            self.share(3, k)

    def on_above(self, k):
        if k == 0:
            super().on_above(k)
        else:
            self.got(self.region(1, k), 3 + k)
            self.share(1, k)

    def on_far(self, k):
        if k == 0:
            super().on_far(k)
            self.put(self.region(2, 0), self.partner, 6)
        else:
            self.got(self.region(2, 1), 6)
            self.share(2, 1)


class RingFirst(Copies):
    def share(self, shift, k):
        self.put(self.region(shift, k), self.sibling, 8 + shift * 2 + k)

    def own(self):
        block = self.region(0, 0)
        self.put(block, self.ring[0], 0)
        self.put(block, self.ring[1], 1)
        self.put(block, self.partner, 4)
        self.share(0, 0)

    def on_below(self):
        self.got(self.region(3, 0), 0)
        self.put(self.region(3, 0, 0), self.ring[0], 2)
        self.put(self.region(3, 0), self.partner, 7)
        self.share(3, 0)

    def on_above(self):
        self.got(self.region(1, 0), 1)
        self.put(self.region(1, 0, 1), self.ring[1], 3)
        self.put(self.region(1, 0), self.partner, 5)
        self.share(1, 0)

    def on_far(self):
        self.got(self.region(2, 0, 0), 2)
        self.got(self.region(2, 0, 1), 3)
        self.put(self.region(2, 0), self.partner, 6)
        self.share(2, 0)

    def on_partner(self, shift):
        self.got(self.region(shift, 1), 4 + shift)
        self.share(shift, 1)

    def wait_shared(self, sibling_region):
        for shift in range(4):
            for k in range(2):
                self.got(sibling_region(shift, k), 8 + shift * 2 + k)


class Views(Copies):
    def own(self):
        block = self.region(0, 0)
        self.put(block, self.partner, 0)
        self.put(block, self.ring[0], 1)
        self.put(block, self.ring[1], 2)

    def on_below(self):
        self.got(self.region(3, 0), 1)
        self.put(self.region(3, 0, 0), self.ring[0], 5)

    def on_above(self):
        self.got(self.region(1, 0), 2)
        self.put(self.region(1, 0, 1), self.ring[1], 6)

    def pass_partner(self):
        block = self.region(0, 1)
        self.got(block, 0)
        self.put(block, self.ring[0], 3)
        self.put(block, self.ring[1], 4)

    def on_far(self):
        self.got(self.region(2, 0, 0), 5)
        self.got(self.region(2, 0, 1), 6)
        self.put(self.region(2, 0), self.partner, 7)

    def last_below(self):
        self.got(self.region(3, 1), 3)

    def last_above(self):
        self.got(self.region(1, 1), 4)

    def last_far(self):
        self.got(self.region(2, 1), 7)


def kernel(
    owner_ref, scale_ref, x_hbm, slot_hbm, gain_ref, w_hbm, wout_hbm, out_ref,
    x_ref, slot_ref, w_ref, tok, ref_tok, wo, kv, query, acc, top, att, att_in, keep, give, moved, arrived,
    t_send, t_recv, s_send, s_recv, s2_send, s2_recv, w_send, w_recv, r_send, r_recv, a_send, a_recv,
    m_send, m_recv, i_sem,
):
    view, seq = lax.axis_index("view"), lax.axis_index("seq")
    x, zl = view // 2, lax.rem(view, 2)
    y, zh, core = seq // 4, lax.rem(seq // 2, 2), lax.rem(seq, 2)

    def seq_of(y_, zh_, c_):
        return (y_ * 2 + zh_) * 2 + c_

    y_up, y_down = lax.rem(y + 1, 4), lax.rem(y + 3, 4)
    x_up, x_down = lax.rem(x + 1, 4), lax.rem(x + 3, 4)
    y_far, x_far = lax.rem(y + 2, 4), lax.rem(x + 2, 4)
    seq_ring = ((view, seq_of(y_up, zh, core)), (view, seq_of(y_down, zh, core)))
    seq_partner = (view, seq_of(y, 1 - zh, core))
    sibling = (view, seq_of(y, zh, 1 - core))
    view_ring = ((x_up * 2 + zl, seq), (x_down * 2 + zl, seq))
    view_partner = (x * 2 + 1 - zl, seq)
    cross = (x * 2 + 1 - zl, seq_of(y, 1 - zh, core))

    peers = []
    for dy in range(4):
        for dz in range(2):
            for dc in range(2):
                if (dy, dz, dc) != (0, 0, 0):
                    zh_ = zh if dz == 0 else 1 - zh
                    c_ = core if dc == 0 else 1 - core
                    peers.append((view, seq_of(lax.rem(y + dy, 4), zh_, c_)))
    peers += [view_partner, view_ring[0], view_ring[1], cross]
    barrier = pltpu.get_barrier_semaphore()
    for peer in peers:
        pl.semaphore_signal(barrier, inc=1, device_id=peer, device_id_type=MESH)

    load_slot = pltpu.make_async_copy(slot_hbm, slot_ref, i_sem.at[0])
    load_x = pltpu.make_async_copy(x_hbm, x_ref, i_sem.at[1])
    load_wo = pltpu.make_async_copy(wout_hbm, wo.at[rows(seq * TB, TB)], i_sem.at[2])
    load_w = [
        pltpu.make_async_copy(w_hbm.at[j], w_ref.at[:, j * HD : (j + 1) * HD], i_sem.at[3 + j])
        for j in range(3)
    ]
    for copy in [load_slot, load_x, load_wo] + load_w:
        copy.start()

    def seq_place(stride, base=0):
        return lambda y_, zh_: seq_of(y_, zh_, core) * stride + base

    me = (y, zh)
    part = SB // 2
    g_t = PartnerFirst(tok, TB, seq_place(TB), me, seq_ring, seq_partner, sibling, t_send, t_recv)
    g_w = FarAcross(wo, TB, seq_place(TB), me, seq_ring, cross, sibling, w_send, w_recv)
    s_ring = RingFirst(ref_tok, part, seq_place(SB), me, seq_ring, seq_partner, sibling, s_send, s_recv)
    s_part = PartnerFirst(
        ref_tok, part, seq_place(SB, part), me, seq_ring, seq_partner, sibling, s2_send, s2_recv
    )
    g_r = Views(
        kv, RC, lambda x_, zl_: (x_ * 2 + zl_) * RC, (x, zl), view_ring, view_partner, None, r_send, r_recv
    )

    def of_sibling(buf, size, stride, base=0):
        def region(shift, k):
            zh_ = zh if k == 0 else 1 - zh
            start = seq_of(lax.rem(y + shift, 4), zh_, 1 - core) * stride + base
            return buf.at[rows(start, size)]

        return region

    slots = [owner_ref[i] for i in range(4)]
    low, high = jnp.int32(99), jnp.int32(-1)
    for slot in slots:
        inner = jnp.logical_and(slot > 0, slot < 7)
        low = jnp.minimum(low, jnp.where(inner, slot, 99))
        high = jnp.maximum(high, jnp.where(inner, slot, -1))
    give_even = jnp.where(
        x == 0, 0, jnp.where(x == 1, (high == 2).astype(jnp.int32), jnp.where(x == 2, (low == 4).astype(jnp.int32), 1))
    )
    for_low = jnp.where(low == 1, 2, jnp.where(low == 2, 0, jnp.where(low == 3, 1, 3)))
    for_high = jnp.where(high == 6, 3, jnp.where(high == 4, 0, jnp.where(high == 5, 1, 2)))
    final = jnp.where(x == 0, 0, jnp.where(x == 1, for_low, jnp.where(x == 2, for_high, 1)))

    gain = gain_ref[...]
    load_slot.wait()
    give[...] = normalise(slot_ref[rows((1 - zl) * SB, SB), :], gain)
    load_x.wait()
    tok[rows(seq * TB, TB), :] = normalise(x_ref[...], gain)
    pl.semaphore_wait(barrier, len(peers))
    parts = [rows(i * part, part) for i in range(2)]

    def swap(i, side):
        return pltpu.make_async_remote_copy(
            src_ref=give.at[parts[i]], dst_ref=keep.at[side, parts[i]],
            send_sem=m_send.at[i], recv_sem=m_recv.at[i],
            device_id=view_partner, device_id_type=MESH,
        )

    half = x // 2

    def move(i, side):
        return pltpu.make_async_remote_copy(
            src_ref=moved.at[parts[i]], dst_ref=arrived.at[side, parts[i]],
            send_sem=m_send.at[2 + i], recv_sem=m_recv.at[2 + 2 * side + i],
            device_id=((x + 1 - 2 * half) * 2 + zl, seq), device_id_type=MESH,
        )

    for i in range(2):
        swap(i, zl).start()
    g_t.own()
    keep[zl] = normalise(slot_ref[rows(zl * SB, SB), :], gain)
    for i in range(2):
        swap(i, 1 - zl).wait_recv()
        moved[parts[i], :] = jnp.where(
            give_even == 1, keep[0, parts[i], :].astype(F32), keep[1, parts[i], :].astype(F32)
        ).astype(BF16)
        move(i, half).start()
    mine = rows(seq * SB, SB)
    middle = jnp.logical_or(x == 1, x == 2)

    @pl.when(jnp.logical_not(middle))
    def _():
        ref_tok[mine, :] = jnp.where(final == 0, keep[0].astype(F32), keep[1].astype(F32)).astype(BF16)

    @pl.when(middle)
    def _():
        for i in range(2):
            for side in range(2):
                move(i, side).wait_recv()
        near = jnp.where(final == 0, keep[0].astype(F32), keep[1].astype(F32))
        far = jnp.where(final == 2, arrived[0].astype(F32), arrived[1].astype(F32))
        ref_tok[mine, :] = jnp.where(final < 2, near, far).astype(BF16)

    factor = scale_ref[0] * (HD ** (-0.5) * math.log2(math.e))

    def project(y_):
        at = rows(y_ * QB, QB)
        qkv = jnp.dot(tok[at, :], w_ref[...], preferred_element_type=F32).astype(BF16)
        kv[rows(4 * LEN + y_ * QB, QB), :] = qkv[:, HD:]
        scaled = qkv[:, :HD].astype(F32) * factor
        high_part = scaled.astype(BF16)
        low_part = (scaled - high_part.astype(F32)).astype(BF16)
        query[at, :] = jnp.concatenate([high_part, low_part], axis=1)

    tok_shared = of_sibling(tok, TB, TB)
    s_ring.own()
    s_part.own()
    g_t.on_below(0)
    g_t.on_above(0)
    s_part.pass_partner()
    s_ring.on_below()
    s_ring.on_above()
    s_part.on_below(0)
    s_part.on_above(0)
    s_ring.on_partner(0)
    s_ring.on_far()
    s_part.on_below(1)
    s_part.on_above(1)
    g_t.pass_partner()
    for copy in load_w:
        copy.wait()
    s_ring.on_partner(1)
    s_ring.on_partner(3)
    s_part.on_far(0)
    s_part.on_far(1)
    s_ring.on_partner(2)
    s_ring.wait_shared(of_sibling(ref_tok, part, SB))
    for shift in range(4):
        s_part.wait_shared(of_sibling(ref_tok, part, SB, part), shift)

    def ref_project(i, _):
        own_kv = jnp.dot(ref_tok[rows(i * QB, QB), :], w_ref[:, HD:], preferred_element_type=F32)
        kv[rows(view * RC + i * QB, QB), :] = own_kv.astype(BF16)
        return 0

    lax.fori_loop(0, RC // QB, ref_project, 0)
    g_r.own()

    begun = set()

    def attend(items, last=None):
        loaded = {}

        def block(t):
            return rows(lax.rem(y + 1 + t, 4) * QB, QB)

        def score(item):
            name, start, size, t = item
            if name not in loaded:
                both = kv[rows(start, size), :]
                loaded[name] = (
                    jnp.concatenate([both[:, :HD], both[:, :HD]], axis=1),
                    jnp.concatenate([both[:, HD:], jnp.ones((size, HD), BF16)], axis=1),
                )
            return lax.dot_general(query[block(t), :], loaded[name][0], NT, preferred_element_type=F32)

        ahead = score(items[0])
        for index, (name, start, size, t) in enumerate(items):
            scores = ahead
            if index + 1 < len(items):
                ahead = score(items[index + 1])
            q = block(t)
            first = t not in begun
            begun.add(t)
            peak = jnp.max(scores, axis=1, keepdims=True)
            if first:
                new = jnp.broadcast_to(peak, (QB, HD))
            else:
                old = top[q, :]
                new = jnp.maximum(old, peak)
            weights = jnp.exp2(scores - jnp.tile(new, (1, size // HD))).astype(BF16)
            total = jnp.dot(weights, loaded[name][1], preferred_element_type=F32)
            if not first:
                total += acc[q, :] * jnp.tile(jnp.exp2(old - new), (1, 2))
            if last:
                att[q, :] = (total[:, :HD] / total[:, HD:]).astype(BF16)
                last(t)
            else:
                top[q, :] = new
                acc[q, :] = total

    sent = []

    def hand_out(t):
        y_ = lax.rem(y + 1 + t, 4)
        for combo in range(4):
            zh_ = zh if combo < 2 else 1 - zh
            c_ = core if combo % 2 == 0 else 1 - core
            to = seq_of(y_, zh_, c_)
            if t == 3 and combo == 0:
                att_in[:, rows(seq * HD, HD)] = att[rows(seq * TB, TB), :]
                continue
            copy = pltpu.make_async_remote_copy(
                src_ref=att.at[rows(to * TB, TB)],
                dst_ref=att_in.at[:, rows(seq * HD, HD)],
                send_sem=a_send.at[t * 4 + combo],
                recv_sem=a_recv.at[t * 4 + combo],
                device_id=(view, to),
                device_id_type=MESH,
            )
            copy.start()
            sent.append(copy)

    def group(x_, zl_):
        return (x_ * 2 + zl_) * RC

    def pair(x_, ts=range(4)):
        return [("pair", group(x_, 0), LEN, t) for t in ts]

    near = (3, 2, 0)
    g_t.wait_shared(tok_shared, 0)
    project(y)
    g_t.on_below(1)
    g_t.on_above(1)
    g_t.on_far(0)
    g_t.wait_shared(tok_shared, 3)
    project(y_down)
    g_t.wait_shared(tok_shared, 1)
    project(y_up)
    attend([("own", group(x, zl), RC, t) for t in near])
    g_r.on_below()
    g_r.on_above()
    g_r.pass_partner()
    g_t.on_far(1)
    load_wo.wait()
    g_w.own()
    attend([("partner", group(x, 1 - zl), RC, t) for t in near])
    g_r.on_far()
    g_t.wait_shared(tok_shared, 2)
    project(y_far)
    attend(pair(x, (1,)) + [("view", 4 * LEN, LEN, t) for t in range(4)])
    g_w.on_below(0)
    g_w.on_above(0)
    g_r.last_below()
    attend(pair(x_down))
    g_w.pass_partner()
    g_r.last_above()
    g_w.on_far(0)
    attend(pair(x_up))
    g_r.last_far()
    attend(pair(x_far), last=hand_out)

    g_w.on_below(1)
    g_w.on_above(1)
    g_w.on_far(1)
    for shift in range(4):
        g_w.wait_shared(of_sibling(wo, TB, TB), shift)
    for t in range(4):
        for combo in range(4):
            if t == 3 and combo == 0:
                continue
            y_ = lax.rem(y + 3 - t, 4)
            zh_ = zh if combo < 2 else 1 - zh
            c_ = core if combo % 2 == 0 else 1 - core
            pltpu.make_async_remote_copy(
                src_ref=att.at[rows(0, TB)],
                dst_ref=att_in.at[:, rows(seq_of(y_, zh_, c_) * HD, HD)],
                send_sem=a_send.at[0],
                recv_sem=a_recv.at[t * 4 + combo],
                device_id=sibling,
                device_id_type=MESH,
            ).wait_recv()

    def output(i, _):
        at = rows(i * QB, QB)
        out_ref[:, at] = jnp.dot(att_in[...], wo[:, at], preferred_element_type=F32).astype(BF16)
        return 0

    lax.fori_loop(0, D // QB, output, 0)
    for i in range(2):
        swap(i, zl).wait_send()
        move(i, half).wait_send()
    for gather in (g_t, s_ring, s_part, g_w, g_r):
        gather.close()
    for copy in sent:
        copy.wait_send()


def local(target, ref_slots, owners, norm_gain, w_qkv, head_scale, w_out):
    vmem = pl.BlockSpec(memory_space=pltpu.VMEM)
    smem = pl.BlockSpec(memory_space=pltpu.SMEM)
    hbm = pl.BlockSpec(memory_space=pl.ANY)
    dma = pltpu.SemaphoreType.DMA
    out = pl.pallas_call(
        kernel,
        out_shape=jax.ShapeDtypeStruct((TB, D), BF16),
        in_specs=[smem, smem, hbm, hbm, vmem, hbm, hbm],
        out_specs=vmem,
        scratch_shapes=[
            pltpu.VMEM((TB, D), BF16),
            pltpu.VMEM((TB, D), BF16),
            pltpu.VMEM((D, 3 * HD), BF16),
            pltpu.VMEM((LEN, D), BF16),
            pltpu.VMEM((RC, D), BF16),
            pltpu.VMEM((D, D), BF16),
            pltpu.VMEM((5 * LEN, 2 * HD), BF16),
            pltpu.VMEM((LEN, 2 * HD), BF16),
            pltpu.VMEM((LEN, 2 * HD), F32),
            pltpu.VMEM((LEN, HD), F32),
            pltpu.VMEM((LEN, HD), BF16),
            pltpu.VMEM((TB, D), BF16),
            pltpu.VMEM((2, SB, D), BF16),
            pltpu.VMEM((SB, D), BF16),
            pltpu.VMEM((SB, D), BF16),
            pltpu.VMEM((2, SB, D), BF16),
            dma((17,)), dma((17,)), dma((16,)), dma((16,)), dma((17,)), dma((17,)), dma((17,)), dma((17,)),
            dma((8,)), dma((8,)), dma((16,)), dma((16,)), dma((4,)), dma((6,)), dma((6,)),
        ],
        compiler_params=pltpu.CompilerParams(
            collective_id=0, has_side_effects=True, vmem_limit_bytes=60 * 2**20
        ),
        cost_estimate=pl.CostEstimate(
            flops=18_000_000_000, bytes_accessed=4_000_000, transcendentals=21_000_000
        ),
    )(
        owners, head_scale, target[0], ref_slots[0], norm_gain[None, :],
        jnp.transpose(w_qkv, (1, 0, 2)), w_out,
    )
    return out[None]


def solution(mesh):
    placed = (
        P("view", "seq", None),
        P("view", "seq", None),
        P(),
        P(),
        P(None, None, "seq"),
        P("seq"),
        P("seq", None),
    )
    return jax.shard_map(
        local, mesh=mesh, in_specs=placed, out_specs=P("view", "seq", None), check_vma=False
    )
```

```python
import math

import jax
import jax.numpy as jnp
from jax import lax
from jax.experimental import pallas as pl
from jax.experimental.pallas import tpu as pltpu
from jax.sharding import PartitionSpec as P

HD = 128
D = 2048
LEN = 2048
TB = 128
SB = 64
RC = 1024
QB = 512
MESH = pl.DeviceIdType.MESH
F32 = jnp.float32
BF16 = jnp.bfloat16
NT = (((1,), (1,)), ((), ()))


def rows(start, size):
    return pl.ds(pl.multiple_of(start, size), size)


def normalise(x, gain):
    xf = x.astype(F32)
    scaled = xf * lax.rsqrt(jnp.mean(xf * xf, axis=-1, keepdims=True) + 1e-06)
    return (scaled * gain).astype(BF16)


class Copies:
    def __init__(self, buf, size, place, me, ring, partner, sibling, send, recv):
        self.buf, self.size, self.place = buf, size, place
        self.pos, self.side = me
        self.ring, self.partner, self.sibling = ring, partner, sibling
        self.send, self.recv = send, recv
        self.started = []

    def region(self, shift, k, half=None):
        pos = lax.rem(self.pos + shift, 4)
        side = self.side if k == 0 else 1 - self.side
        start = self.place(pos, side)
        if half is None:
            return self.buf.at[rows(start, self.size)]
        part = self.size // 2
        return self.buf.at[rows(start + half * part, part)]

    def put(self, region, device, sem):
        copy = pltpu.make_async_remote_copy(
            src_ref=region,
            dst_ref=region,
            send_sem=self.send.at[len(self.started)],
            recv_sem=self.recv.at[sem],
            device_id=device,
            device_id_type=MESH,
        )
        copy.start()
        self.started.append(copy)

    def got(self, region, sem):
        pltpu.make_async_remote_copy(
            src_ref=region,
            dst_ref=region,
            send_sem=self.send.at[0],
            recv_sem=self.recv.at[sem],
            device_id=self.partner,
            device_id_type=MESH,
        ).wait_recv()

    def close(self):
        for copy in self.started:
            copy.wait_send()


class PartnerFirst(Copies):
    def share(self, shift, k):
        self.put(self.region(shift, k), self.sibling, 9 + {0: 0, 3: 2, 1: 4, 2: 6}[shift] + k)

    def own(self):
        block = self.region(0, 0)
        self.put(block, self.ring[0], 1)
        self.put(block, self.ring[1], 3)
        self.put(block, self.partner, 0)
        self.share(0, 0)

    def pass_partner(self):
        block = self.region(0, 1)
        self.got(block, 0)
        self.put(block, self.ring[0], 2)
        self.put(block, self.ring[1], 4)
        self.share(0, 1)

    def on_below(self, k):
        self.got(self.region(3, k), 1 + k)
        self.put(self.region(3, k, 0), self.ring[0], 5 + k)
        self.share(3, k)

    def on_above(self, k):
        self.got(self.region(1, k), 3 + k)
        self.put(self.region(1, k, 1), self.ring[1], 7 + k)
        self.share(1, k)

    def on_far(self, k):
        self.got(self.region(2, k, 0), 5 + k)
        self.got(self.region(2, k, 1), 7 + k)
        self.share(2, k)

    def wait_shared(self, sibling_region, shift):
        for k in range(2):
            self.got(sibling_region(shift, k), 9 + {0: 0, 3: 2, 1: 4, 2: 6}[shift] + k)


class FarAcross(PartnerFirst):
    def on_below(self, k):
        if k == 0:
            super().on_below(k)
        else:
            self.got(self.region(3, k), 1 + k)
            self.share(3, k)

    def on_above(self, k):
        if k == 0:
            super().on_above(k)
        else:
            self.got(self.region(1, k), 3 + k)
            self.share(1, k)

    def on_far(self, k):
        if k == 0:
            super().on_far(k)
            self.put(self.region(2, 0), self.partner, 6)
        else:
            self.got(self.region(2, 1), 6)
            self.share(2, 1)


class RingFirst(Copies):
    def share(self, shift, k):
        self.put(self.region(shift, k), self.sibling, 8 + shift * 2 + k)

    def own(self):
        block = self.region(0, 0)
        self.put(block, self.ring[0], 0)
        self.put(block, self.ring[1], 1)
        self.put(block, self.partner, 4)
        self.share(0, 0)

    def on_below(self):
        self.got(self.region(3, 0), 0)
        self.put(self.region(3, 0, 0), self.ring[0], 2)
        self.put(self.region(3, 0), self.partner, 7)
        self.share(3, 0)

    def on_above(self):
        self.got(self.region(1, 0), 1)
        self.put(self.region(1, 0, 1), self.ring[1], 3)
        self.put(self.region(1, 0), self.partner, 5)
        self.share(1, 0)

    def on_far(self):
        self.got(self.region(2, 0, 0), 2)
        self.got(self.region(2, 0, 1), 3)
        self.put(self.region(2, 0), self.partner, 6)
        self.share(2, 0)

    def on_partner(self, shift):
        self.got(self.region(shift, 1), 4 + shift)
        self.share(shift, 1)

    def wait_shared(self, sibling_region):
        for shift in range(4):
            for k in range(2):
                self.got(sibling_region(shift, k), 8 + shift * 2 + k)


class Views(Copies):
    def own(self):
        block = self.region(0, 0)
        self.put(block, self.partner, 0)
        self.put(block, self.ring[0], 1)
        self.put(block, self.ring[1], 2)

    def on_below(self):
        self.got(self.region(3, 0), 1)
        self.put(self.region(3, 0, 0), self.ring[0], 5)

    def on_above(self):
        self.got(self.region(1, 0), 2)
        self.put(self.region(1, 0, 1), self.ring[1], 6)

    def pass_partner(self):
        block = self.region(0, 1)
        self.got(block, 0)
        self.put(block, self.ring[0], 3)
        self.put(block, self.ring[1], 4)

    def on_far(self):
        self.got(self.region(2, 0, 0), 5)
        self.got(self.region(2, 0, 1), 6)
        self.put(self.region(2, 0), self.partner, 7)

    def last_below(self):
        self.got(self.region(3, 1), 3)

    def last_above(self):
        self.got(self.region(1, 1), 4)

    def last_far(self):
        self.got(self.region(2, 1), 7)


def kernel(
    owner_ref, scale_ref, x_hbm, slot_hbm, gain_ref, w_hbm, wout_hbm, out_ref,
    x_ref, slot_ref, w_ref, tok, ref_tok, wo, kv, query, acc, top, att, att_in, keep, give, moved, arrived,
    t_send, t_recv, s_send, s_recv, s2_send, s2_recv, w_send, w_recv, r_send, r_recv, a_send, a_recv,
    m_send, m_recv, i_sem,
):
    view, seq = lax.axis_index("view"), lax.axis_index("seq")
    x, zl = view // 2, lax.rem(view, 2)
    y, zh, core = seq // 4, lax.rem(seq // 2, 2), lax.rem(seq, 2)

    def seq_of(y_, zh_, c_):
        return (y_ * 2 + zh_) * 2 + c_

    y_up, y_down = lax.rem(y + 1, 4), lax.rem(y + 3, 4)
    x_up, x_down = lax.rem(x + 1, 4), lax.rem(x + 3, 4)
    y_far, x_far = lax.rem(y + 2, 4), lax.rem(x + 2, 4)
    seq_ring = ((view, seq_of(y_up, zh, core)), (view, seq_of(y_down, zh, core)))
    seq_partner = (view, seq_of(y, 1 - zh, core))
    sibling = (view, seq_of(y, zh, 1 - core))
    view_ring = ((x_up * 2 + zl, seq), (x_down * 2 + zl, seq))
    view_partner = (x * 2 + 1 - zl, seq)
    cross = (x * 2 + 1 - zl, seq_of(y, 1 - zh, core))

    peers = []
    for dy in range(4):
        for dz in range(2):
            for dc in range(2):
                if (dy, dz, dc) != (0, 0, 0):
                    zh_ = zh if dz == 0 else 1 - zh
                    c_ = core if dc == 0 else 1 - core
                    peers.append((view, seq_of(lax.rem(y + dy, 4), zh_, c_)))
    peers += [view_partner, view_ring[0], view_ring[1], cross]
    barrier = pltpu.get_barrier_semaphore()
    for peer in peers:
        pl.semaphore_signal(barrier, inc=1, device_id=peer, device_id_type=MESH)

    load_slot = pltpu.make_async_copy(slot_hbm, slot_ref, i_sem.at[0])
    load_x = pltpu.make_async_copy(x_hbm, x_ref, i_sem.at[1])
    load_wo = pltpu.make_async_copy(wout_hbm, wo.at[rows(seq * TB, TB)], i_sem.at[2])
    load_w = [
        pltpu.make_async_copy(w_hbm.at[j], w_ref.at[:, j * HD : (j + 1) * HD], i_sem.at[3 + j])
        for j in range(3)
    ]
    for copy in [load_slot, load_x, load_wo] + load_w:
        copy.start()

    def seq_place(stride, base=0):
        return lambda y_, zh_: seq_of(y_, zh_, core) * stride + base

    me = (y, zh)
    part = SB // 2
    g_t = PartnerFirst(tok, TB, seq_place(TB), me, seq_ring, seq_partner, sibling, t_send, t_recv)
    g_w = FarAcross(wo, TB, seq_place(TB), me, seq_ring, cross, sibling, w_send, w_recv)
    s_ring = RingFirst(ref_tok, part, seq_place(SB), me, seq_ring, seq_partner, sibling, s_send, s_recv)
    s_part = PartnerFirst(
        ref_tok, part, seq_place(SB, part), me, seq_ring, seq_partner, sibling, s2_send, s2_recv
    )
    g_r = Views(
        kv, RC, lambda x_, zl_: (x_ * 2 + zl_) * RC, (x, zl), view_ring, view_partner, None, r_send, r_recv
    )

    def of_sibling(buf, size, stride, base=0):
        def region(shift, k):
            zh_ = zh if k == 0 else 1 - zh
            start = seq_of(lax.rem(y + shift, 4), zh_, 1 - core) * stride + base
            return buf.at[rows(start, size)]

        return region

    slots = [owner_ref[i] for i in range(4)]
    low, high = jnp.int32(99), jnp.int32(-1)
    for slot in slots:
        inner = jnp.logical_and(slot > 0, slot < 7)
        low = jnp.minimum(low, jnp.where(inner, slot, 99))
        high = jnp.maximum(high, jnp.where(inner, slot, -1))
    give_even = jnp.where(
        x == 0, 0, jnp.where(x == 1, (high == 2).astype(jnp.int32), jnp.where(x == 2, (low == 4).astype(jnp.int32), 1))
    )
    for_low = jnp.where(low == 1, 2, jnp.where(low == 2, 0, jnp.where(low == 3, 1, 3)))
    for_high = jnp.where(high == 6, 3, jnp.where(high == 4, 0, jnp.where(high == 5, 1, 2)))
    final = jnp.where(x == 0, 0, jnp.where(x == 1, for_low, jnp.where(x == 2, for_high, 1)))

    gain = gain_ref[...]
    load_slot.wait()
    give[...] = normalise(slot_ref[rows((1 - zl) * SB, SB), :], gain)
    load_x.wait()
    tok[rows(seq * TB, TB), :] = normalise(x_ref[...], gain)
    pl.semaphore_wait(barrier, len(peers))
    parts = [rows(i * part, part) for i in range(2)]

    def swap(i, side):
        return pltpu.make_async_remote_copy(
            src_ref=give.at[parts[i]], dst_ref=keep.at[side, parts[i]],
            send_sem=m_send.at[i], recv_sem=m_recv.at[i],
            device_id=view_partner, device_id_type=MESH,
        )

    half = x // 2

    def move(i, side):
        return pltpu.make_async_remote_copy(
            src_ref=moved.at[parts[i]], dst_ref=arrived.at[side, parts[i]],
            send_sem=m_send.at[2 + i], recv_sem=m_recv.at[2 + 2 * side + i],
            device_id=((x + 1 - 2 * half) * 2 + zl, seq), device_id_type=MESH,
        )

    for i in range(2):
        swap(i, zl).start()
    g_t.own()
    keep[zl] = normalise(slot_ref[rows(zl * SB, SB), :], gain)
    for i in range(2):
        swap(i, 1 - zl).wait_recv()
        moved[parts[i], :] = jnp.where(
            give_even == 1, keep[0, parts[i], :].astype(F32), keep[1, parts[i], :].astype(F32)
        ).astype(BF16)
        move(i, half).start()
    mine = rows(seq * SB, SB)
    middle = jnp.logical_or(x == 1, x == 2)

    @pl.when(jnp.logical_not(middle))
    def _():
        ref_tok[mine, :] = jnp.where(final == 0, keep[0].astype(F32), keep[1].astype(F32)).astype(BF16)

    @pl.when(middle)
    def _():
        for i in range(2):
            for side in range(2):
                move(i, side).wait_recv()
        near = jnp.where(final == 0, keep[0].astype(F32), keep[1].astype(F32))
        far = jnp.where(final == 2, arrived[0].astype(F32), arrived[1].astype(F32))
        ref_tok[mine, :] = jnp.where(final < 2, near, far).astype(BF16)

    factor = scale_ref[0] * (HD ** (-0.5) * math.log2(math.e))

    def project(y_):
        at = rows(y_ * QB, QB)
        qkv = jnp.dot(tok[at, :], w_ref[...], preferred_element_type=F32).astype(BF16)
        kv[rows(4 * LEN + y_ * QB, QB), :] = qkv[:, HD:]
        scaled = qkv[:, :HD].astype(F32) * factor
        high_part = scaled.astype(BF16)
        low_part = (scaled - high_part.astype(F32)).astype(BF16)
        query[at, :] = jnp.concatenate([high_part, low_part], axis=1)

    tok_shared = of_sibling(tok, TB, TB)
    s_ring.own()
    s_part.own()
    g_t.on_below(0)
    g_t.on_above(0)
    s_part.pass_partner()
    s_ring.on_below()
    s_ring.on_above()
    s_part.on_below(0)
    s_part.on_above(0)
    s_ring.on_partner(0)
    s_ring.on_far()
    s_part.on_below(1)
    s_part.on_above(1)
    g_t.pass_partner()
    for copy in load_w:
        copy.wait()
    s_ring.on_partner(1)
    s_ring.on_partner(3)
    s_part.on_far(0)
    s_part.on_far(1)
    s_ring.on_partner(2)
    s_ring.wait_shared(of_sibling(ref_tok, part, SB))
    for shift in range(4):
        s_part.wait_shared(of_sibling(ref_tok, part, SB, part), shift)

    def ref_project(i, _):
        own_kv = jnp.dot(ref_tok[rows(i * QB, QB), :], w_ref[:, HD:], preferred_element_type=F32)
        kv[rows(view * RC + i * QB, QB), :] = own_kv.astype(BF16)
        return 0

    lax.fori_loop(0, RC // QB, ref_project, 0)
    g_r.own()

    begun = set()

    def attend(items, last=None):
        loaded = {}

        def block(t):
            return rows(lax.rem(y + 1 + t, 4) * QB, QB)

        def score(item):
            name, start, size, t = item
            if name not in loaded:
                both = kv[rows(start, size), :]
                loaded[name] = (
                    jnp.concatenate([both[:, :HD], both[:, :HD]], axis=1),
                    jnp.concatenate([both[:, HD:], jnp.ones((size, HD), BF16)], axis=1),
                )
            return lax.dot_general(query[block(t), :], loaded[name][0], NT, preferred_element_type=F32)

        ahead = score(items[0])
        for index, (name, start, size, t) in enumerate(items):
            scores = ahead
            if index + 1 < len(items):
                ahead = score(items[index + 1])
            q = block(t)
            first = t not in begun
            begun.add(t)
            peak = jnp.max(scores, axis=1, keepdims=True)
            if first:
                new = jnp.broadcast_to(peak, (QB, HD))
            else:
                old = top[q, :]
                new = jnp.maximum(old, peak)
            weights = jnp.exp2(scores - jnp.tile(new, (1, size // HD))).astype(BF16)
            total = jnp.dot(weights, loaded[name][1], preferred_element_type=F32)
            if not first:
                total += acc[q, :] * jnp.tile(jnp.exp2(old - new), (1, 2))
            if last:
                att[q, :] = (total[:, :HD] / total[:, HD:]).astype(BF16)
                last(t)
            else:
                top[q, :] = new
                acc[q, :] = total

    sent = []

    def hand_out(t):
        y_ = lax.rem(y + 1 + t, 4)
        for combo in range(4):
            zh_ = zh if combo < 2 else 1 - zh
            c_ = core if combo % 2 == 0 else 1 - core
            to = seq_of(y_, zh_, c_)
            if t == 3 and combo == 0:
                att_in[:, rows(seq * HD, HD)] = att[rows(seq * TB, TB), :]
                continue
            copy = pltpu.make_async_remote_copy(
                src_ref=att.at[rows(to * TB, TB)],
                dst_ref=att_in.at[:, rows(seq * HD, HD)],
                send_sem=a_send.at[t * 4 + combo],
                recv_sem=a_recv.at[t * 4 + combo],
                device_id=(view, to),
                device_id_type=MESH,
            )
            copy.start()
            sent.append(copy)

    def group(x_, zl_):
        return (x_ * 2 + zl_) * RC

    def pair(x_, ts=range(4)):
        return [("pair", group(x_, 0), LEN, t) for t in ts]

    near = (3, 2, 0)
    g_t.wait_shared(tok_shared, 0)
    project(y)
    g_t.on_below(1)
    g_t.on_above(1)
    g_t.on_far(0)
    g_t.wait_shared(tok_shared, 3)
    project(y_down)
    g_t.wait_shared(tok_shared, 1)
    project(y_up)
    attend([("own", group(x, zl), RC, t) for t in near])
    g_r.on_below()
    g_r.on_above()
    g_r.pass_partner()
    g_t.on_far(1)
    load_wo.wait()
    g_w.own()
    attend([("partner", group(x, 1 - zl), RC, t) for t in near])
    g_r.on_far()
    g_t.wait_shared(tok_shared, 2)
    project(y_far)
    attend(pair(x, (1,)) + [("view", 4 * LEN, LEN, t) for t in range(4)])
    g_w.on_below(0)
    g_w.on_above(0)
    g_r.last_below()
    attend(pair(x_down))
    g_w.pass_partner()
    g_r.last_above()
    g_w.on_far(0)
    attend(pair(x_up))
    g_r.last_far()
    attend(pair(x_far), last=hand_out)

    g_w.on_below(1)
    g_w.on_above(1)
    g_w.on_far(1)
    for shift in range(4):
        g_w.wait_shared(of_sibling(wo, TB, TB), shift)
    for t in range(4):
        for combo in range(4):
            if t == 3 and combo == 0:
                continue
            y_ = lax.rem(y + 3 - t, 4)
            zh_ = zh if combo < 2 else 1 - zh
            c_ = core if combo % 2 == 0 else 1 - core
            pltpu.make_async_remote_copy(
                src_ref=att.at[rows(0, TB)],
                dst_ref=att_in.at[:, rows(seq_of(y_, zh_, c_) * HD, HD)],
                send_sem=a_send.at[0],
                recv_sem=a_recv.at[t * 4 + combo],
                device_id=sibling,
                device_id_type=MESH,
            ).wait_recv()

    def output(i, _):
        at = rows(i * QB, QB)
        out_ref[:, at] = jnp.dot(att_in[...], wo[:, at], preferred_element_type=F32).astype(BF16)
        return 0

    lax.fori_loop(0, D // QB, output, 0)
    for i in range(2):
        swap(i, zl).wait_send()
        move(i, half).wait_send()
    for gather in (g_t, s_ring, s_part, g_w, g_r):
        gather.close()
    for copy in sent:
        copy.wait_send()


def local(target, ref_slots, owners, norm_gain, w_qkv, head_scale, w_out):
    vmem = pl.BlockSpec(memory_space=pltpu.VMEM)
    smem = pl.BlockSpec(memory_space=pltpu.SMEM)
    hbm = pl.BlockSpec(memory_space=pl.ANY)
    dma = pltpu.SemaphoreType.DMA
    out = pl.pallas_call(
        kernel,
        out_shape=jax.ShapeDtypeStruct((TB, D), BF16),
        in_specs=[smem, smem, hbm, hbm, vmem, hbm, hbm],
        out_specs=vmem,
        scratch_shapes=[
            pltpu.VMEM((TB, D), BF16),
            pltpu.VMEM((TB, D), BF16),
            pltpu.VMEM((D, 3 * HD), BF16),
            pltpu.VMEM((LEN, D), BF16),
            pltpu.VMEM((RC, D), BF16),
            pltpu.VMEM((D, D), BF16),
            pltpu.VMEM((5 * LEN, 2 * HD), BF16),
            pltpu.VMEM((LEN, 2 * HD), BF16),
            pltpu.VMEM((LEN, 2 * HD), F32),
            pltpu.VMEM((LEN, HD), F32),
            pltpu.VMEM((LEN, HD), BF16),
            pltpu.VMEM((TB, D), BF16),
            pltpu.VMEM((2, SB, D), BF16),
            pltpu.VMEM((SB, D), BF16),
            pltpu.VMEM((SB, D), BF16),
            pltpu.VMEM((2, SB, D), BF16),
            dma((17,)), dma((17,)), dma((16,)), dma((16,)), dma((17,)), dma((17,)), dma((17,)), dma((17,)),
            dma((8,)), dma((8,)), dma((16,)), dma((16,)), dma((4,)), dma((6,)), dma((6,)),
        ],
        compiler_params=pltpu.CompilerParams(
            collective_id=0, has_side_effects=True, vmem_limit_bytes=60 * 2**20
        ),
        cost_estimate=pl.CostEstimate(
            flops=18_000_000_000, bytes_accessed=4_000_000, transcendentals=21_000_000
        ),
    )(
        owners, head_scale, target[0], ref_slots[0], norm_gain[None, :],
        jnp.transpose(w_qkv, (1, 0, 2)), w_out,
    )
    return out[None]


def solution(mesh):
    placed = (
        P("view", "seq", None),
        P("view", "seq", None),
        P(),
        P(),
        P(None, None, "seq"),
        P("seq"),
        P("seq", None),
    )
    return jax.shard_map(
        local, mesh=mesh, in_specs=placed, out_specs=P("view", "seq", None), check_vma=False
    )
```
